1024 devices in a mesh: dp: 16 (over x, y_lo, core), space: 64 (over y_hi, z).
Axes of the slice: x: 4, y: 4 (y_hi: 2, y_lo: 2; y = y_hi * 2 + y_lo), z: 32, core: 2. Of those that a mesh axis runs over, the one named last changes fastest.
Arguments:
- inputs: bfloat16 [16, 64, 24, 4608], P('dp', 'space'), may hold values from -6 to 6
- cotangent: bfloat16 [16, 64, 24, 4608], P('dp', 'space'), may hold values from -16 to 16
- tile_rows: int32 [64], replicated, may hold values from 4 to 24, as said below
- neighbour_step: int32 [64, 4], replicated, may hold values from -1 to 1
- neighbour_code: int32 [64, 4], replicated, may hold values from 0 to 7
- neighbour_shift: int32 [64, 4], replicated, may hold values from -6 to 6
- conv_kernel: float32 [7, 7, 192], replicated, may hold values from -0.875 to 0.875
- conv_bias: float32 [192], replicated, may hold values from -3 to 3
- norm_gain: float32 [192], replicated, may hold values from 0.5 to 1.5
- norm_bias: float32 [192], replicated, may hold values from -3 to 3
- w_expand: bfloat16 [192, 768], replicated, may hold values from -0.4375 to 0.4375
- b_expand: float32 [768], replicated, may hold values from -3 to 3
- w_project: bfloat16 [768, 192], replicated, may hold values from -0.21875 to 0.21875
- b_project: float32 [192], replicated, may hold values from -3 to 3
- layer_scale: float32 [192], replicated, may hold values from 0.5 to 1.5
Outputs:
- outputs: bfloat16 [16, 64, 24, 4608], P('dp', 'space')
- input_grad: bfloat16 [16, 64, 24, 4608], P('dp', 'space')
- weight_grads: float32 [294912], P(('dp', 'space'))
The draws below stay inside these ranges and needn't reach their ends.
Inputs may be any that keep to these rules, and one draw needn't show every extreme that they name: `tile_rows`: tile t and tile t + 32 hold 28 rows together; tile 0 holds 24 rows.
All inputs are finite; a program needn't handle non-finite values.
Results may differ from the reference program's by a relative error of at most 0.023.
Values may be sent and summed in bfloat16 or wider, within the bound.
A program may use at most 32 MiB of HBM per device.

```python
import math
import jax
import jax.numpy as jnp
from jax import lax

C = 192
H = 768
KERNEL = 7
TS = 24
ROWS_MIN = 4
REACH = 1
SAMPLES = 16
TILES = 64


def draw_tile_rows(key, part):
    leading = jax.random.randint(key, (TILES // 2,), ROWS_MIN, TS + 1)
    leading = leading.at[0].set(TS)
    return jnp.concatenate([leading, TS + ROWS_MIN - leading]).astype(jnp.int32)


def place_ends(drawn, own_key, smallest, top_value):
    longest = drawn.shape.index(max(drawn.shape))
    spots = []
    for shift in (0, 1):
        where = [jax.random.randint(jax.random.fold_in(own_key, axis), (), 0, length) for axis, length in enumerate(drawn.shape)]
        where[longest] = (where[longest] + shift) % drawn.shape[longest]
        spots.append(tuple(where))
    return drawn.at[spots[0]].set(smallest).at[spots[1]].set(top_value)


def spiked(values, key, source, target, shards_of, factor):
    owner, partner = [(jnp.arange(values.shape[position]) // (values.shape[position] // shards_of)).reshape([-1 if axis == position else 1 for axis in range(values.ndim)]) for position in (source, target)]
    chosen = jax.random.permutation(key, shards_of)[partner]
    strong = (owner == chosen) | (owner == (partner + shards_of // 2) % shards_of)
    return jnp.where(strong, factor * values, values)


def block_levels(stream_key, dims, split, smallest, top_value):
    def one(axis_at, blocks):
        draws = jax.random.uniform(jax.random.fold_in(jax.random.fold_in(stream_key, 6), axis_at), (blocks,), jnp.float32, smallest / len(split), top_value / len(split))
        return jnp.repeat(jnp.exp(draws), dims[axis_at] // blocks).reshape((-1,) + (1,) * (len(dims) - axis_at - 1))

    loudness = one(*split[0])
    for cut in split[1:]:
        loudness = loudness * one(*cut)
    return loudness


def gaussian(rng, shape, scale, bound, split=(), kind=jnp.bfloat16):
    values = jax.random.normal(rng, shape, jnp.float32) * scale
    if len(split) > 0:
        values = block_levels(rng, shape, split, -0.22, 0.18) * values
    return jnp.clip(values, min=-bound, max=bound).astype(kind)


def noise_with(stream_key, shape, deviation, bound, split, heavy, held_as=jnp.bfloat16):
    values = deviation * jax.random.normal(stream_key, shape, jnp.float32)
    if split:
        values = values * block_levels(stream_key, shape, split, -0.22, 0.18)
    return jnp.clip(spiked(values, jax.random.fold_in(stream_key, 3), *heavy), -bound, bound).astype(held_as)


def setup_inputs(seed: int = 0) -> dict:
    seeds = jax.random.split(jax.random.key(seed), 16)
    return {
        "inputs": gaussian(seeds[0], (SAMPLES, TILES, TS, TS * C), 1.0, 6.0, ((0, 16), (1, 64))),
        "cotangent": noise_with(seeds[1], (SAMPLES, TILES, TS, TS * C), 1.0, 16.0, ((0, 16), (1, 64)), (1, 3, 64, 4.0)),
        "tile_rows": draw_tile_rows(jax.random.fold_in(seeds[15], 71), 0),
        "neighbour_step": place_ends(jax.random.randint(seeds[3], (TILES, 4), 0 - REACH, REACH + 1), jax.random.fold_in(seeds[3], 1), 0 - REACH, REACH).astype(jnp.int32),
        "neighbour_code": place_ends(jax.random.randint(seeds[4], (TILES, 4), 0, 8), jax.random.fold_in(seeds[4], 1), 0, 7).astype(jnp.int32),
        "neighbour_shift": place_ends(jax.random.randint(seeds[5], (TILES, 4), 0 - TS // 4, TS // 4 + 1), jax.random.fold_in(seeds[5], 1), 0 - TS // 4, (TS // 4 + 1) - 1).astype(jnp.int32),
        "conv_kernel": gaussian(seeds[6], (KERNEL, KERNEL, C), (KERNEL * KERNEL) ** -0.5, 0.875, (), jnp.float32),
        "conv_bias": gaussian(seeds[7], (C,), 0.5, 3.0, (), jnp.float32),
        "norm_gain": jnp.clip(1.0 + 0.1 * jax.random.normal(seeds[8], (C,), jnp.float32), 0.5, 1.5),
        "norm_bias": gaussian(seeds[9], (C,), 0.3, 3.0, (), jnp.float32),
        "w_expand": gaussian(seeds[10], (C, H), C ** -0.5, 0.4375),
        "b_expand": gaussian(seeds[11], (H,), 0.5, 3.0, (), jnp.float32),
        "w_project": gaussian(seeds[12], (H, C), H ** -0.5, 0.21875),
        "b_project": gaussian(seeds[13], (C,), 0.3, 3.0, (), jnp.float32),
        "layer_scale": jnp.clip(1.0 + 0.1 * jax.random.normal(seeds[14], (C,), jnp.float32), 0.5, 1.5),
    }


root_half = 0.7071067811865476
inv_root_tau = 0.3989422804014327

def gelu_exact(values):
    return 0.5 * values * (1.0 + jax.scipy.special.erf(values * root_half))

def gelu_slope(values):
    return 0.5 * (1.0 + jax.scipy.special.erf(values * root_half)) + values * inv_root_tau * jnp.exp(-0.5 * values * values)

def tile_bands(tile_field, tile_len):
    tile_side = tile_field.shape[0]
    upper = tile_field[0:3]
    bottom_rows = tile_len - 1 - jnp.arange(3, dtype=jnp.int32)
    bottom = jnp.take(tile_field, bottom_rows, axis=0)
    leftmost = jnp.transpose(tile_field[:, 0:3], (1, 0, 2))
    rightmost = jnp.transpose(tile_field[:, tile_side - 3:][:, ::-1], (1, 0, 2))
    return jnp.stack([upper, bottom, leftmost, rightmost])

def orient_band(band_rows, orient_code, edge_shift):
    tile_side = band_rows.shape[1]
    flipped = jnp.where(orient_code % 2 == 1, band_rows[:, ::-1], band_rows)
    padded = jnp.pad(flipped, ((0, 0), (tile_side, tile_side), (0, 0)))
    return lax.dynamic_slice_in_dim(padded, tile_side - edge_shift, tile_side, 1)

def restore_band(band_rows, orient_code, edge_shift):
    tile_side = band_rows.shape[1]
    padded = jnp.pad(band_rows, ((0, 0), (tile_side, tile_side), (0, 0)))
    moved = lax.dynamic_slice_in_dim(padded, tile_side + edge_shift, tile_side, 1)
    return jnp.where(orient_code % 2 == 1, moved[:, ::-1], moved)

def extend_tile(tile_field, tile_len, halos):
    tile_side = tile_field.shape[0]
    channels = tile_field.shape[2]
    extended = jnp.zeros((tile_side + 6, tile_side + 6, channels), tile_field.dtype)
    extended = extended.at[3:tile_side + 3, 3:tile_side + 3].set(tile_field)
    extended = extended.at[0:3, 3:tile_side + 3].set(halos[0][::-1])
    extended = extended.at[3:tile_side + 3, 0:3].set(jnp.transpose(halos[2], (1, 0, 2))[:, ::-1])
    extended = extended.at[3:tile_side + 3, tile_side + 3:tile_side + 6].set(jnp.transpose(halos[3], (1, 0, 2)))
    zero_index = tile_len * 0
    return lax.dynamic_update_slice(extended, halos[1], (tile_len + 3, zero_index + 3, zero_index))

def halo_grads(grad_ext, tile_len):
    tile_side = grad_ext.shape[0] - 6
    channels = grad_ext.shape[2]
    zero_index = tile_len * 0
    upper = grad_ext[0:3, 3:tile_side + 3][::-1]
    bottom = lax.dynamic_slice(grad_ext, (tile_len + 3, zero_index + 3, zero_index), (3, tile_side, channels))
    leftmost = jnp.transpose(grad_ext[3:tile_side + 3, 0:3][:, ::-1], (1, 0, 2))
    rightmost = jnp.transpose(grad_ext[3:tile_side + 3, tile_side + 3:tile_side + 6], (1, 0, 2))
    return jnp.stack([upper, bottom, leftmost, rightmost])

def band_adjoint(grad_bands, tile_len):
    tile_side = grad_bands.shape[2]
    channels = grad_bands.shape[3]
    result = jnp.zeros((tile_side, tile_side, channels), jnp.float32)
    result = result.at[0:3].add(grad_bands[0])
    bottom_rows = tile_len - 1 - jnp.arange(3, dtype=jnp.int32)
    result = result.at[bottom_rows].add(grad_bands[1])
    result = result.at[:, 0:3].add(jnp.transpose(grad_bands[2], (1, 0, 2)))
    result = result.at[:, tile_side - 3:].add(jnp.transpose(grad_bands[3], (1, 0, 2))[:, ::-1])
    return result

def depthwise(extended, conv_kernel):
    channels = conv_kernel.shape[-1]
    return lax.conv_general_dilated(extended, conv_kernel[:, :, None, :], (1, 1), 'VALID', dimension_numbers=('NHWC', 'HWIO', 'NHWC'), feature_group_count=channels, precision=lax.Precision.HIGHEST)

def layer_norm(values, norm_gain, norm_bias):
    centred = values - lax.optimization_barrier(jnp.mean(values, axis=-1, keepdims=True))
    variance = lax.optimization_barrier(jnp.mean(centred * centred, axis=-1, keepdims=True))
    return centred * lax.rsqrt(variance + 1e-06) * norm_gain + norm_bias

def pointwise(cells, d_cells, w_expand, b_expand, w_project, b_project):
    pre = jnp.dot(cells, w_expand, preferred_element_type=jnp.float32) + b_expand
    act = gelu_exact(pre).astype(jnp.bfloat16)
    branch = (jnp.dot(act, w_project, preferred_element_type=jnp.float32) + b_project).astype(jnp.bfloat16)
    d_act = lax.dot_general(d_cells, w_project, (((1,), (1,)), ((), ())), preferred_element_type=jnp.float32)
    d_pre = (d_act * gelu_slope(pre)).astype(jnp.bfloat16)
    d_normed = lax.dot_general(d_pre, w_expand, (((1,), (1,)), ((), ())), preferred_element_type=jnp.float32).astype(jnp.bfloat16)
    grad_in = lax.dot_general(cells, d_pre, (((0,), (0,)), ((), ())), preferred_element_type=jnp.float32)
    grad_proj = lax.dot_general(act, d_cells, (((0,), (0,)), ((), ())), preferred_element_type=jnp.float32)
    return (branch, d_normed, grad_in, grad_proj)

def reference(inputs, cotangent, tile_rows, neighbour_step, neighbour_code, neighbour_shift, conv_kernel, conv_bias, norm_gain, norm_bias, w_expand, b_expand, w_project, b_project, layer_scale):
    samples, tiles, tile_side = (inputs.shape[0], inputs.shape[1], inputs.shape[2])
    channels = conv_kernel.shape[-1]
    inside = (jnp.arange(tile_side, dtype=jnp.int32)[None, :] < tile_rows[:, None])[:, :, None, None]
    sources = (jnp.arange(tiles, dtype=jnp.int32)[:, None] + neighbour_step) % tiles
    sides = neighbour_code // 2

    def one_sample(pair):
        sample_in, sample_cot = pair
        tile_field = sample_in.reshape(tiles, tile_side, tile_side, channels)
        tile_field = jnp.where(inside, tile_field, jnp.zeros((), jnp.bfloat16))
        bands = jax.vmap(tile_bands)(tile_field, tile_rows)
        picked = bands[sources, sides]
        halos = jax.vmap(jax.vmap(orient_band))(picked, neighbour_code, neighbour_shift)
        extended = jax.vmap(extend_tile)(tile_field, tile_rows, halos).astype(jnp.float32)
        mixed = depthwise(extended, conv_kernel) + conv_bias
        normed_f, norm_pull = jax.vjp(lambda values: layer_norm(values, norm_gain, norm_bias), mixed)
        normed = normed_f.astype(jnp.bfloat16)
        grad_out = jnp.where(inside, sample_cot.reshape(tiles, tile_side, tile_side, channels).astype(jnp.float32), 0.0)
        d_branch = (layer_scale * grad_out).astype(jnp.bfloat16)
        branch, d_normed, grad_in, grad_proj = pointwise(normed.reshape(-1, channels), d_branch.reshape(-1, channels), w_expand, b_expand, w_project, b_project)
        branch = branch.reshape(tiles, tile_side, tile_side, channels)
        outputs = jnp.where(inside, tile_field.astype(jnp.float32) + layer_scale * branch.astype(jnp.float32), 0.0)
        d_mixed = norm_pull(d_normed.reshape(mixed.shape).astype(jnp.float32))[0]
        conv_pull = jax.vjp(lambda values: depthwise(values, conv_kernel), extended)[1]
        grad_ext = conv_pull(d_mixed)[0]
        grad_halos = jax.vmap(halo_grads)(grad_ext, tile_rows)
        returned = jax.vmap(jax.vmap(restore_band))(grad_halos, neighbour_code, neighbour_shift).astype(jnp.bfloat16)
        segment_ids = (sources * 4 + sides).reshape(-1)
        grad_bands = jax.ops.segment_sum(returned.reshape(tiles * 4, -1).astype(jnp.float32), segment_ids, num_segments=tiles * 4).reshape(tiles, 4, 3, tile_side, channels)
        d_field = grad_out + grad_ext[:, 3:tile_side + 3, 3:tile_side + 3] + jax.vmap(band_adjoint)(grad_bands, tile_rows)
        input_grad = jnp.where(inside, d_field, 0.0)
        return (outputs.astype(jnp.bfloat16).reshape(tiles, tile_side, tile_side * channels), input_grad.astype(jnp.bfloat16).reshape(tiles, tile_side, tile_side * channels), grad_in, grad_proj)
    outputs, input_grad, grad_in, grad_proj = lax.map(one_sample, (inputs, cotangent))
    scale = 1.0 / math.sqrt(samples * tiles * tile_side * tile_side)
    weight_grads = jnp.concatenate([lax.optimization_barrier(jnp.sum(grad_in, axis=0)).reshape(-1), lax.optimization_barrier(jnp.sum(grad_proj, axis=0)).reshape(-1)]) * scale
    return (outputs, input_grad, weight_grads)
```

```python
import math

import jax
import jax.numpy as jnp
from jax import lax
from jax.experimental import pallas as pl
from jax.experimental.pallas import tpu as pltpu
from jax.sharding import PartitionSpec as P

C = 192
H = 768
TS = 24
CELLS = TS * TS
TILES = 64
SAMPLES = 16
WIDE = TS * C
PAIR = 2 * C
ROOT_HALF = 0.7071067811865476
INV_ROOT_TAU = 0.3989422804014327
SCALE = 1.0 / math.sqrt(SAMPLES * TILES * CELLS)
F32 = jnp.float32
BF16 = jnp.bfloat16
MESH = pl.DeviceIdType.MESH
SMEM = pl.BlockSpec(memory_space=pltpu.SMEM)
VMEM = pl.BlockSpec(memory_space=pltpu.VMEM)


def iota(shape, dim):
    return lax.broadcasted_iota(jnp.int32, shape, dim)


def one_hot(found, wanted):
    return jnp.where(found == wanted, 1.0, 0.0).astype(BF16)


def dot(a, b):
    return jnp.dot(a, b, preferred_element_type=F32)


def dot_tb(a, b):
    return lax.dot_general(a, b, (((1,), (1,)), ((), ())), preferred_element_type=F32)


def dot_ta(a, b):
    return lax.dot_general(a, b, (((0,), (0,)), ((), ())), preferred_element_type=F32)


def columns_of(ref):
    columns = []
    for p in range(TS // 2):
        pair = ref[:, p * PAIR : (p + 1) * PAIR].astype(F32)
        columns += [pair[:, :C], pair[:, C:]]
    return columns


def band_cells(tile_len):
    i = iota((TS, 1), 0)
    parts = []
    for k in range(3):
        parts.append(i * TS + k)
        parts.append(i * TS + (tile_len - 1 - k))
        parts.append(jnp.where(i < tile_len, k * TS + i, -1))
        parts.append(jnp.where(i < tile_len, (TS - 1 - k) * TS + i, -1))
    return parts


def oriented(position, code, shift):
    unshifted = position - shift
    index = jnp.where(code % 2 == 1, TS - 1 - unshifted, unshifted)
    return index, (unshifted >= 0) & (unshifted < TS)


def bands_kernel(
    rows_ref, step_ref, code_ref, shift_ref, x_ref, halo_ref, own, from_lo, from_hi, send, recv
):
    me = lax.axis_index("space")
    dp = lax.axis_index("dp")
    hi = lax.rem(me + 1, TILES)
    lo = lax.rem(me + TILES - 1, TILES)
    barrier = pltpu.get_barrier_semaphore()
    for peer in (lo, hi):
        pl.semaphore_signal(barrier, inc=1, device_id=(dp, peer), device_id_type=MESH)
    cells = jnp.concatenate(columns_of(x_ref), axis=0).astype(BF16)
    wanted = jnp.concatenate(band_cells(rows_ref[me]), axis=0)
    own[...] = dot(one_hot(iota((288, CELLS), 1), wanted), cells).astype(BF16)
    pl.semaphore_wait(barrier, 2)
    copies = []
    for n, (peer, landing) in enumerate(((hi, from_lo), (lo, from_hi))):
        copy = pltpu.make_async_remote_copy(
            src_ref=own,
            dst_ref=landing,
            send_sem=send.at[n],
            recv_sem=recv.at[n],
            device_id=(dp, peer),
            device_id_type=MESH,
        )
        copy.start()
        copies.append(copy)
    position = iota((TS, 1), 0)
    picks = []
    for source in range(3):
        parts = []
        for q in range(4):
            code = code_ref[q, me]
            index, on_band = oriented(position, code, shift_ref[q, me])
            first = jnp.where(step_ref[q, me] + 1 == source, (code // 2) * TS, -1000)
            parts.append(jnp.where(on_band, first + index, -1))
        picks.append(one_hot(iota((96, 96), 1), jnp.concatenate(parts, axis=0)))
    for copy in copies:
        copy.wait()
    for k in range(3):
        rows = slice(96 * k, 96 * k + 96)
        halo_ref[rows, :] = (
            dot(picks[0], from_lo[rows, :])
            + dot(picks[1], own[rows, :])
            + dot(picks[2], from_hi[rows, :])
        ).astype(BF16)


def block_kernel(
    rows_ref,
    x_ref,
    c_ref,
    halo_ref,
    kern_ref,
    bias_ref,
    gain_ref,
    shift_ref,
    we_ref,
    be_ref,
    wp_ref,
    bp_ref,
    ls_ref,
    out_ref,
    base_ref,
    dh_ref,
    gi_ref,
    gp_ref,
    weights,
    ext,
    ext_at,
    mixed,
    normal,
    rstd,
    normed,
    d_branch,
    branch,
    d_normed,
    d_pad,
    d_at,
    d_ext,
):
    tile_len = rows_ref[lax.axis_index("space")]
    inside = iota((TS, C), 0) < tile_len
    for t in range(49):
        weights[t] = jnp.broadcast_to(kern_ref[t : t + 1, :], (8, C))

    halo = halo_ref[...].astype(F32)
    col = iota((1, 144), 1)
    target = col
    for m in range(6):
        row = (7 - m // 2) if m % 2 == 0 else (tile_len + 8 + m // 2)
        target = jnp.where(col >= TS * m, col * 40 + (row - 960 * m), target)
    edge_rows = jnp.concatenate([halo[96 * k : 96 * k + 48] for k in range(3)], axis=0).astype(BF16)
    ext[3:27] = dot(one_hot(iota((960, 144), 0), target), edge_rows).reshape(TS, 40, C)
    blank = jnp.zeros((40, C), F32)
    for k in range(3):
        ext[2 - k] = blank
        ext[27 + k] = blank
        ext[2 - k, 8:32] = halo[96 * k + 48 : 96 * k + 72]
        ext[27 + k, 8:32] = halo[96 * k + 72 : 96 * k + 96]
    for j, column in enumerate(columns_of(x_ref)):
        ext[3 + j, 8:32] += jnp.where(inside, column, 0.0)

    @pl.loop(0, 30)
    def _(at):
        whole = ext[at]
        for a in range(7):
            ext_at[a, at] = whole[5 + a : 29 + a]

    @pl.loop(0, 6)
    def _(block):
        first = block * 4
        totals = [jnp.broadcast_to(bias_ref[...], (TS, C)) for _ in range(4)]
        for a in range(7):
            for column in range(10):
                value = ext_at[a, first + column].reshape(3, 8, C)
                for j in range(4):
                    b = column - j
                    if 0 <= b < 7:
                        totals[j] = totals[j] + (value * weights[7 * a + b][None]).reshape(TS, C)
        for j in range(4):
            mixed[pl.ds((first + j) * TS, TS), :] = totals[j]

    @pl.loop(0, 6)
    def _(block):
        rows = pl.ds(pl.multiple_of(block * 96, 96), 96)
        value = mixed[rows, :]
        centred = value - jnp.mean(value, axis=1, keepdims=True)
        inverse = lax.rsqrt(jnp.mean(centred * centred, axis=1, keepdims=True) + 1e-06)
        scaled = centred * inverse
        normal[rows, :] = scaled
        rstd[rows, :] = jnp.broadcast_to(inverse, (96, 128))
        normed[rows, :] = (scaled * gain_ref[...] + shift_ref[...]).astype(BF16)

    grads = [jnp.where(inside, column, 0.0) for column in columns_of(c_ref)]
    for j in range(TS):
        base_ref[j * TS : j * TS + TS, :] = grads[j]
    d_branch[...] = (base_ref[...] * ls_ref[...]).astype(BF16)

    grad_in, grad_proj = [], []
    for chunk in range(3):
        hidden = slice(256 * chunk, 256 * chunk + 256)
        pre = dot(normed[...], we_ref[:, hidden]) + be_ref[:, hidden]
        phi = 0.5 * (1.0 + lax.erf(pre * ROOT_HALF))
        act = (pre * phi).astype(BF16)
        slope = phi + pre * INV_ROOT_TAU * jnp.exp(-0.5 * pre * pre)
        d_act = dot_tb(d_branch[...], wp_ref[hidden, :])
        d_pre = (d_act * slope).astype(BF16)
        forward = dot(act, wp_ref[hidden, :])
        backward = dot_tb(d_pre, we_ref[:, hidden])
        if chunk == 0:
            branch[...] = forward
            d_normed[...] = backward
        else:
            branch[...] += forward
            d_normed[...] += backward
        grad_in.append(dot_ta(normed[...], d_pre) * SCALE)
        grad_proj.append(dot_ta(act, d_branch[...]) * SCALE)
    grad_in = jnp.concatenate(grad_in, axis=1)
    grad_proj = jnp.concatenate(grad_proj, axis=0)
    for core in range(2):
        for x in range(2):
            gi_ref[core, x] = jnp.concatenate(
                [grad_in[24 * d : 24 * d + 24] for d in (4 * x + core, 4 * x + 2 + core)], axis=0
            ).astype(BF16)
            gp_ref[core, x] = jnp.concatenate(
                [grad_proj[96 * d : 96 * d + 96] for d in (4 * x + core, 4 * x + 2 + core)], axis=1
            ).astype(BF16)

    for p, (left, right) in enumerate(zip(*[iter(columns_of(x_ref))] * 2)):
        pair = []
        for j, column in ((2 * p, left), (2 * p + 1, right)):
            value = (branch[j * TS : j * TS + TS, :] + bp_ref[...]).astype(BF16).astype(F32)
            pair.append(jnp.where(inside, column + ls_ref[...] * value, 0.0))
        out_ref[:, p * PAIR : (p + 1) * PAIR] = jnp.concatenate(pair, axis=1).astype(BF16)

    d_pad[...] = jnp.zeros_like(d_pad)

    @pl.loop(0, 6)
    def _(block):
        rows = pl.ds(pl.multiple_of(block * 96, 96), 96)
        grad = d_normed[rows, :].astype(BF16).astype(F32) * gain_ref[...]
        scaled = normal[rows, :]
        mean = jnp.mean(grad, axis=1, keepdims=True)
        along = jnp.mean(grad * scaled, axis=1, keepdims=True)
        value = rstd[rows, 0:1] * (grad - mean - scaled * along)
        for j in range(4):
            d_pad[block * 4 + j + 6, 8:32] = value[j * TS : j * TS + TS]

    @pl.loop(0, 36)
    def _(at):
        whole = d_pad[at]
        for a in range(7):
            d_at[a, at] = whole[8 - a : 40 - a]

    @pl.loop(0, 10)
    def _(block):
        first = block * 3
        totals = [jnp.zeros((32, C), F32) for _ in range(3)]
        for a in range(7):
            for column in range(9):
                value = d_at[a, first + column].reshape(4, 8, C)
                for j in range(3):
                    b = j - column + 6
                    if 0 <= b < 7:
                        totals[j] = totals[j] + (value * weights[7 * a + b][None]).reshape(32, C)
        for j in range(3):
            d_ext[first + j] = totals[j]

    parts = []
    j = iota((TS, 1), 0)
    for m in range(6):
        parts.append(j * 32 + ((2 - m // 2) if m % 2 == 0 else (tile_len + 3 + m // 2)))
    middle = d_ext[3:27].reshape(TS * 32, C).astype(BF16)
    edge_rows = dot(one_hot(iota((144, TS * 32), 1), jnp.concatenate(parts, axis=0)), middle)
    parts = []
    for k in range(3):
        parts += [
            edge_rows[48 * k : 48 * k + 48],
            d_ext[2 - k, 3:27],
            d_ext[27 + k, 3:27],
        ]
    dh_ref[...] = jnp.concatenate(parts, axis=0).astype(BF16)
    for j in range(TS):
        base_ref[j * TS : j * TS + TS, :] += d_ext[3 + j, 3:27]


def finish_kernel(
    rows_ref,
    step_ref,
    code_ref,
    shift_ref,
    gi_ref,
    gp_ref,
    dh_ref,
    base_ref,
    ig_ref,
    wg_ref,
    dh_lo,
    dh_hi,
    core_i,
    core_p,
    xs_i,
    xs_p,
    xr_i,
    xr_p,
    ys_i,
    ys_p,
    yr_i,
    yr_p,
    hs_i,
    hs_p,
    hr_i,
    hr_p,
    ls_i,
    ls_p,
    lr_i,
    lr_p,
    own_x_i,
    own_x_p,
    own_y_i,
    own_y_p,
    own_h_i,
    own_h_p,
    dh_send,
    dh_recv,
    core_send,
    core_recv,
    x_send,
    x_recv,
    y_send,
    y_recv,
    h_send,
    h_recv,
    l_send,
    l_recv,
):
    me = lax.axis_index("space")
    dp = lax.axis_index("dp")
    mx = dp // 4
    core = lax.rem(dp, 2)
    my = (me // 32) * 2 + lax.rem(dp // 2, 2)
    z = lax.rem(me, 32)
    mh = z // 8
    ml = lax.rem(z, 8)
    hi = lax.rem(me + 1, TILES)
    lo = lax.rem(me + TILES - 1, TILES)
    other = dp + 1 - 2 * core

    def at_x(x):
        return (x * 4 + lax.rem(dp, 4), me)

    def at_y(y):
        return (mx * 4 + lax.rem(y, 2) * 2 + core, (y // 2) * 32 + z)

    def at_h(h):
        return (dp, (me // 32) * 32 + h * 8 + ml)

    def at_l(lane):
        return (dp, (me // 8) * 8 + lane)

    xs = [lax.rem(mx + d, 4) for d in (1, 2, 3)]
    ys = [lax.rem(my + d, 4) for d in (1, 2, 3)]
    hs = [lax.rem(mh + d, 4) for d in (1, 2, 3)]
    lanes = [lax.rem(ml + d, 8) for d in range(1, 8)]
    peers = [(dp, lo), (dp, hi), (other, me)]
    peers += [at_x(x) for x in xs] + [at_y(y) for y in ys]
    peers += [at_h(h) for h in hs] + [at_l(lane) for lane in lanes]
    barrier = pltpu.get_barrier_semaphore()
    for peer in peers:
        pl.semaphore_signal(barrier, inc=1, device_id=peer, device_id_type=MESH)
    pl.semaphore_wait(barrier, len(peers))

    def remote(source, landing, send, recv, peer):
        return pltpu.make_async_remote_copy(
            src_ref=source,
            dst_ref=landing,
            send_sem=send,
            recv_sem=recv,
            device_id=peer,
            device_id_type=MESH,
        )

    core_copies = [
        remote(gi_ref.at[1 - core], core_i, core_send.at[0], core_recv.at[0], (other, me)),
        remote(gp_ref.at[1 - core], core_p, core_send.at[1], core_recv.at[1], (other, me)),
    ]
    dh_copies = [
        remote(dh_ref, dh_lo, dh_send.at[0], dh_recv.at[0], (dp, hi)),
        remote(dh_ref, dh_hi, dh_send.at[1], dh_recv.at[1], (dp, lo)),
    ]
    for copy in core_copies + dh_copies:
        copy.start()
    for copy in core_copies:
        copy.wait()
    for x in range(2):
        sum_i = gi_ref[core, x].astype(F32) + core_i[x].astype(F32)
        sum_p = gp_ref[core, x].astype(F32) + core_p[x].astype(F32)
        own_x_i[x] = sum_i
        own_x_p[x] = sum_p
        xs_i[x] = sum_i.astype(BF16)
        xs_p[x] = sum_p.astype(BF16)

    def x_copy(n, x, wide):
        if wide:
            return remote(xs_i.at[x], xr_i.at[n], x_send.at[n], x_recv.at[n], at_x(x))
        return remote(xs_p.at[x - 2], xr_p.at[n], x_send.at[n], x_recv.at[n], at_x(x))

    for n, x in enumerate(xs):

        @pl.when(x < 2)
        def _():
            x_copy(n, x, True).start()

        @pl.when(x >= 2)
        def _():
            x_copy(n, x, False).start()

    tile_len = rows_ref[me]
    spread = []
    lane = iota((1, 96), 1)
    for source in range(3):
        sender = lax.rem(me + source + TILES - 1, TILES)
        target = jnp.full((1, 96), -1, jnp.int32)
        for q in range(4):
            code = code_ref[q, sender]
            index, on_band = oriented(lane - TS * q, code, shift_ref[q, sender])
            first = jnp.where(step_ref[q, sender] == 1 - source, (code // 2) * TS, -1000)
            mine = (lane >= TS * q) & (lane < TS * q + TS)
            target = jnp.where(mine & on_band, first + index, target)
        spread.append(one_hot(iota((96, 96), 0), target))
    cell = jnp.concatenate(band_cells(tile_len), axis=0)
    to_bands = one_hot(iota((288, CELLS), 1), cell)
    for copy in dh_copies:
        copy.wait()
    parts = []
    for k in range(3):
        rows = slice(96 * k, 96 * k + 96)
        parts.append(
            dot(spread[0], dh_lo[rows, :])
            + dot(spread[1], dh_ref[rows, :])
            + dot(spread[2], dh_hi[rows, :])
        )
    d_bands = jnp.concatenate(parts, axis=0)
    upper = d_bands.astype(BF16)
    lower = (d_bands - upper.astype(F32)).astype(BF16)
    total = base_ref[...] + (dot_ta(to_bands, upper) + dot_ta(to_bands, lower))
    inside = iota((TS, PAIR), 0) < tile_len
    for p in range(TS // 2):
        pair = [total[j * TS : j * TS + TS] for j in (2 * p, 2 * p + 1)]
        ig_ref[:, p * PAIR : (p + 1) * PAIR] = jnp.where(
            inside, jnp.concatenate(pair, axis=1), 0.0
        ).astype(BF16)

    def exchange(peers_at, send_refs, recv_ref, send, recv):
        copies = []
        for n, (source, device) in enumerate(zip(send_refs, peers_at)):
            copies.append(remote(source, recv_ref.at[n], send.at[n], recv.at[n], device))
        for copy in copies:
            copy.start()
        for copy in copies:
            copy.wait()

    def tail(wide, own_x, xr, own_y, ysend, yr, own_h, hsend, hr, lsend, lr):
        total = own_x[mx if wide else mx - 2]
        for n in range(3):
            total = total + xr[n].astype(F32)
        count = 12 if wide else 48
        for y in range(4):
            if wide:
                part = total[24 * (y % 2) + 12 * (y // 2) :][:12]
            else:
                part = total[48 * (y // 2) :][:48, C * (y % 2) :][:, :C]
            own_y[y, 0:count] = part
            ysend[y, 0:count] = part.astype(BF16)
        exchange([at_y(y) for y in ys], [ysend.at[y] for y in ys], yr, y_send, y_recv)
        total = own_y[my, 0:count]
        for n in range(3):
            total = total + yr[n, 0:count].astype(F32)
        count = count // 4
        for h in range(4):
            part = total[h * count : h * count + count]
            own_h[h, 0:count] = part
            hsend[h, 0:count] = part.astype(BF16)
        exchange([at_h(h) for h in hs], [hsend.at[h] for h in hs], hr, h_send, h_recv)
        total = own_h[mh, 0:count]
        for n in range(3):
            total = total + hr[n, 0:count].astype(F32)
        lsend[0:count] = total.astype(BF16)
        exchange([at_l(lane) for lane in lanes], [lsend] * 7, lr, l_send, l_recv)
        for n in range(7):
            total = total + lr[n, 0:count].astype(F32)
        width = total.shape[1]
        for m in range(8):
            pieces, at = [], 288 * m
            while at < 288 * m + 288:
                row, first = at // width, at % width
                size = min(288 * m + 288 - at, width - first)
                pieces.append(total[row : row + 1, first : first + size])
                at += size

            @pl.when(ml == m)
            def _():
                wg_ref[...] = jnp.concatenate(pieces, axis=1) if len(pieces) > 1 else pieces[0]

    @pl.when(mx < 2)
    def _():
        for n, x in enumerate(xs):
            remote(xs_i.at[0], xr_i.at[n], x_send.at[n], x_recv.at[n], at_x(x)).wait_recv()
        tail(True, own_x_i, xr_i, own_y_i, ys_i, yr_i, own_h_i, hs_i, hr_i, ls_i, lr_i)

    @pl.when(mx >= 2)
    def _():
        for n, x in enumerate(xs):
            remote(xs_p.at[0], xr_p.at[n], x_send.at[n], x_recv.at[n], at_x(x)).wait_recv()
        tail(False, own_x_p, xr_p, own_y_p, ys_p, yr_p, own_h_p, hs_p, hr_p, ls_p, lr_p)

    for n, x in enumerate(xs):

        @pl.when(x < 2)
        def _():
            x_copy(n, x, True).wait_send()

        @pl.when(x >= 2)
        def _():
            x_copy(n, x, False).wait_send()


def local(
    inputs,
    cotangent,
    tile_rows,
    neighbour_step,
    neighbour_code,
    neighbour_shift,
    conv_kernel,
    conv_bias,
    norm_gain,
    norm_bias,
    w_expand,
    b_expand,
    w_project,
    b_project,
    layer_scale,
):
    x = inputs.reshape(TS, WIDE)
    c = cotangent.reshape(TS, WIDE)
    tables = (neighbour_step.T, neighbour_code.T, neighbour_shift.T)
    dma = pltpu.SemaphoreType.DMA
    halo = pl.pallas_call(
        bands_kernel,
        out_shape=jax.ShapeDtypeStruct((288, C), BF16),
        in_specs=[SMEM] * 4 + [VMEM],
        out_specs=VMEM,
        scratch_shapes=[pltpu.VMEM((288, C), BF16)] * 3 + [dma((2,)), dma((2,))],
        compiler_params=pltpu.CompilerParams(
            collective_id=0, has_side_effects=True, vmem_limit_bytes=16 << 20
        ),
        name="bands",
    )(tile_rows, *tables, x)
    out, base, dh, gi, gp = pl.pallas_call(
        block_kernel,
        out_shape=(
            jax.ShapeDtypeStruct((TS, WIDE), BF16),
            jax.ShapeDtypeStruct((CELLS, C), F32),
            jax.ShapeDtypeStruct((288, C), BF16),
            jax.ShapeDtypeStruct((2, 2, 48, H), BF16),
            jax.ShapeDtypeStruct((2, 2, 96, PAIR), BF16),
        ),
        in_specs=[SMEM] + [VMEM] * 12,
        out_specs=(VMEM,) * 5,
        scratch_shapes=[
            pltpu.VMEM((49, 8, C), F32),
            pltpu.VMEM((30, 40, C), F32),
            pltpu.VMEM((7, 30, TS, C), F32),
            pltpu.VMEM((CELLS, C), F32),
            pltpu.VMEM((CELLS, C), F32),
            pltpu.VMEM((CELLS, 128), F32),
            pltpu.VMEM((CELLS, C), BF16),
            pltpu.VMEM((CELLS, C), BF16),
            pltpu.VMEM((CELLS, C), F32),
            pltpu.VMEM((CELLS, C), F32),
            pltpu.VMEM((36, 40, C), F32),
            pltpu.VMEM((7, 36, 32, C), F32),
            pltpu.VMEM((30, 32, C), F32),
        ],
        compiler_params=pltpu.CompilerParams(vmem_limit_bytes=48 << 20),
        name="block",
    )(
        tile_rows,
        x,
        c,
        halo,
        conv_kernel.reshape(49, C),
        conv_bias.reshape(1, C),
        norm_gain.reshape(1, C),
        norm_bias.reshape(1, C),
        w_expand,
        b_expand.reshape(1, H),
        w_project,
        b_project.reshape(1, C),
        layer_scale.reshape(1, C),
    )
    vm = pltpu.VMEM
    ig, wg = pl.pallas_call(
        finish_kernel,
        out_shape=(
            jax.ShapeDtypeStruct((TS, WIDE), BF16),
            jax.ShapeDtypeStruct((1, 288), F32),
        ),
        in_specs=[SMEM] * 4 + [VMEM] * 4,
        out_specs=(VMEM, VMEM),
        scratch_shapes=[
            vm((288, C), BF16),
            vm((288, C), BF16),
            vm((2, 48, H), BF16),
            vm((2, 96, PAIR), BF16),
            vm((2, 48, H), BF16),
            vm((2, 96, PAIR), BF16),
            vm((3, 48, H), BF16),
            vm((3, 96, PAIR), BF16),
            vm((4, 16, H), BF16),
            vm((4, 48, C), BF16),
            vm((3, 16, H), BF16),
            vm((3, 48, C), BF16),
            vm((4, 16, H), BF16),
            vm((4, 16, C), BF16),
            vm((3, 16, H), BF16),
            vm((3, 16, C), BF16),
            vm((16, H), BF16),
            vm((16, C), BF16),
            vm((7, 16, H), BF16),
            vm((7, 16, C), BF16),
            vm((2, 48, H), F32),
            vm((2, 96, PAIR), F32),
            vm((4, 16, H), F32),
            vm((4, 48, C), F32),
            vm((4, 16, H), F32),
            vm((4, 16, C), F32),
        ]
        + [dma((2,))] * 4
        + [dma((3,))] * 6
        + [dma((7,))] * 2,
        compiler_params=pltpu.CompilerParams(
            collective_id=1, has_side_effects=True, vmem_limit_bytes=32 << 20
        ),
        name="finish",
    )(tile_rows, *tables, gi, gp, dh, base)
    return (
        out.reshape(1, 1, TS, WIDE),
        ig.reshape(1, 1, TS, WIDE),
        wg.reshape(288),
    )


def solution(mesh):
    field = P("dp", "space", None, None)
    return jax.shard_map(
        local,
        mesh=mesh,
        in_specs=(field, field) + (P(),) * 13,
        out_specs=(field, field, P(("dp", "space"))),
        check_vma=False,
    )
```

```python
import math

import jax
import jax.numpy as jnp
from jax import lax
from jax.experimental import pallas as pl
from jax.experimental.pallas import tpu as pltpu
from jax.sharding import PartitionSpec as P

C = 192
H = 768
TS = 24
CELLS = TS * TS
TILES = 64
SAMPLES = 16
WIDE = TS * C
PAIR = 2 * C
ROOT_HALF = 0.7071067811865476
INV_ROOT_TAU = 0.3989422804014327
SCALE = 1.0 / math.sqrt(SAMPLES * TILES * CELLS)
F32 = jnp.float32
BF16 = jnp.bfloat16
MESH = pl.DeviceIdType.MESH
SMEM = pl.BlockSpec(memory_space=pltpu.SMEM)
VMEM = pl.BlockSpec(memory_space=pltpu.VMEM)


def iota(shape, dim):
    return lax.broadcasted_iota(jnp.int32, shape, dim)


def one_hot(found, wanted):
    return jnp.where(found == wanted, 1.0, 0.0).astype(BF16)


def dot(a, b):
    return jnp.dot(a, b, preferred_element_type=F32)


def dot_tb(a, b):
    return lax.dot_general(a, b, (((1,), (1,)), ((), ())), preferred_element_type=F32)


def dot_ta(a, b):
    return lax.dot_general(a, b, (((0,), (0,)), ((), ())), preferred_element_type=F32)


def columns_of(ref):
    columns = []
    for p in range(TS // 2):
        pair = ref[:, p * PAIR : (p + 1) * PAIR].astype(F32)
        columns += [pair[:, :C], pair[:, C:]]
    return columns


def band_cells(tile_len):
    i = iota((TS, 1), 0)
    parts = []
    for k in range(3):
        parts.append(i * TS + k)
        parts.append(i * TS + (tile_len - 1 - k))
        parts.append(jnp.where(i < tile_len, k * TS + i, -1))
        parts.append(jnp.where(i < tile_len, (TS - 1 - k) * TS + i, -1))
    return parts


def oriented(position, code, shift):
    unshifted = position - shift
    index = jnp.where(code % 2 == 1, TS - 1 - unshifted, unshifted)
    return index, (unshifted >= 0) & (unshifted < TS)


def bands_kernel(
    rows_ref, step_ref, code_ref, shift_ref, x_ref, halo_ref, own, from_lo, from_hi, send, recv
):
    me = lax.axis_index("space")
    dp = lax.axis_index("dp")
    hi = lax.rem(me + 1, TILES)
    lo = lax.rem(me + TILES - 1, TILES)
    barrier = pltpu.get_barrier_semaphore()
    for peer in (lo, hi):
        pl.semaphore_signal(barrier, inc=1, device_id=(dp, peer), device_id_type=MESH)
    cells = jnp.concatenate(columns_of(x_ref), axis=0).astype(BF16)
    wanted = jnp.concatenate(band_cells(rows_ref[me]), axis=0)
    own[...] = dot(one_hot(iota((288, CELLS), 1), wanted), cells).astype(BF16)
    pl.semaphore_wait(barrier, 2)
    copies = []
    for n, (peer, landing) in enumerate(((hi, from_lo), (lo, from_hi))):
        copy = pltpu.make_async_remote_copy(
            src_ref=own,
            dst_ref=landing,
            send_sem=send.at[n],
            recv_sem=recv.at[n],
            device_id=(dp, peer),
            device_id_type=MESH,
        )
        copy.start()
        copies.append(copy)
    position = iota((TS, 1), 0)
    picks = []
    for source in range(3):
        parts = []
        for q in range(4):
            code = code_ref[q, me]
            index, on_band = oriented(position, code, shift_ref[q, me])
            first = jnp.where(step_ref[q, me] + 1 == source, (code // 2) * TS, -1000)
            parts.append(jnp.where(on_band, first + index, -1))
        picks.append(one_hot(iota((96, 96), 1), jnp.concatenate(parts, axis=0)))
    for copy in copies:
        copy.wait()
    for k in range(3):
        rows = slice(96 * k, 96 * k + 96)
        halo_ref[rows, :] = (
            dot(picks[0], from_lo[rows, :])
            + dot(picks[1], own[rows, :])
            + dot(picks[2], from_hi[rows, :])
        ).astype(BF16)


def main_kernel(
    rows_ref,
    step_ref,
    code_ref,
    shift_ref,
    x_ref,
    c_ref,
    halo_ref,
    kern_ref,
    bias_ref,
    gain_ref,
    nbias_ref,
    we_ref,
    be_ref,
    wp_ref,
    bp_ref,
    ls_ref,
    out_ref,
    ig_ref,
    wg_ref,
    weights,
    ext,
    ext_at,
    mixed,
    normal,
    rstd,
    normed,
    d_branch,
    branch,
    d_normed,
    d_pad,
    d_at,
    d_ext,
    base_ref,
    dh_ref,
    gi_ref,
    gp_ref,
    dh_lo,
    dh_hi,
    core_i,
    core_p,
    xs_i,
    xs_p,
    xr_i,
    xr_p,
    own_x_i,
    own_x_p,
    y_send_buf,
    y_recv_buf,
    z_send_buf,
    z_recv_buf,
    dh_send,
    dh_recv,
    core_send,
    core_recv,
    x_send,
    x_recv,
    y_send,
    y_recv,
    z_send,
    z_recv,
):
    me = lax.axis_index("space")
    dp = lax.axis_index("dp")
    mx = dp // 4
    core = lax.rem(dp, 2)
    my = (me // 32) * 2 + lax.rem(dp // 2, 2)
    z = lax.rem(me, 32)
    hi = lax.rem(me + 1, TILES)
    lo = lax.rem(me + TILES - 1, TILES)
    other = dp + 1 - 2 * core

    def at_x(x):
        return (x * 4 + lax.rem(dp, 4), me)

    def at_y(y):
        return (mx * 4 + lax.rem(y, 2) * 2 + core, (y // 2) * 32 + z)

    def at_z(other_z):
        return (dp, me - z + other_z)

    xs = [lax.rem(mx + d, 4) for d in (1, 2, 3)]
    ys = [lax.rem(my + d, 4) for d in (1, 2, 3)]
    far_first = sorted(range(1, 32), key=lambda d: -min(d, 32 - d))
    zs = [lax.rem(z + d, 32) for d in far_first]
    peers = [at_z(other_z) for other_z in zs] + [at_y(y) for y in ys] + [at_x(x) for x in xs]
    peers += [(dp, lo), (dp, hi), (other, me)]
    barrier = pltpu.get_barrier_semaphore()
    for peer in peers:
        pl.semaphore_signal(barrier, inc=1, device_id=peer, device_id_type=MESH)

    def remote(source, landing, send, recv, peer):
        return pltpu.make_async_remote_copy(
            src_ref=source,
            dst_ref=landing,
            send_sem=send,
            recv_sem=recv,
            device_id=peer,
            device_id_type=MESH,
        )

    tile_len = rows_ref[me]
    inside = iota((TS, C), 0) < tile_len
    for t in range(49):
        weights[t] = jnp.broadcast_to(kern_ref[t // 7, t % 7 : t % 7 + 1, :], (8, C))

    halo = halo_ref[...].astype(F32)
    col = iota((1, 144), 1)
    target = col
    for m in range(6):
        row = (7 - m // 2) if m % 2 == 0 else (tile_len + 8 + m // 2)
        target = jnp.where(col >= TS * m, col * 40 + (row - 960 * m), target)
    edge_rows = jnp.concatenate([halo[96 * k : 96 * k + 48] for k in range(3)], axis=0).astype(BF16)
    ext[3:27] = dot(one_hot(iota((960, 144), 0), target), edge_rows).reshape(TS, 40, C)
    blank = jnp.zeros((40, C), F32)
    for k in range(3):
        ext[2 - k] = blank
        ext[27 + k] = blank
        ext[2 - k, 8:32] = halo[96 * k + 48 : 96 * k + 72]
        ext[27 + k, 8:32] = halo[96 * k + 72 : 96 * k + 96]
    for j, column in enumerate(columns_of(x_ref)):
        ext[3 + j, 8:32] += jnp.where(inside, column, 0.0)

    @pl.loop(0, 30)
    def _(at):
        whole = ext[at]
        for a in range(7):
            ext_at[a, at] = whole[5 + a : 29 + a]

    @pl.loop(0, 6)
    def _(block):
        first = block * 4
        totals = [jnp.broadcast_to(bias_ref[...], (TS, C)) for _ in range(4)]
        for a in range(7):
            for column in range(10):
                value = ext_at[a, first + column].reshape(3, 8, C)
                for j in range(4):
                    b = column - j
                    if 0 <= b < 7:
                        totals[j] = totals[j] + (value * weights[7 * a + b][None]).reshape(TS, C)
        for j in range(4):
            mixed[pl.ds((first + j) * TS, TS), :] = totals[j]

    @pl.loop(0, 6)
    def _(block):
        rows = pl.ds(pl.multiple_of(block * 96, 96), 96)
        value = mixed[rows, :]
        centred = value - jnp.mean(value, axis=1, keepdims=True)
        inverse = lax.rsqrt(jnp.mean(centred * centred, axis=1, keepdims=True) + 1e-06)
        scaled = centred * inverse
        normal[rows, :] = scaled
        rstd[rows, :] = jnp.broadcast_to(inverse, (96, 128))
        normed[rows, :] = (scaled * gain_ref[...] + nbias_ref[...]).astype(BF16)

    grads = [jnp.where(inside, column, 0.0) for column in columns_of(c_ref)]
    for j in range(TS):
        base_ref[j * TS : j * TS + TS, :] = grads[j]
    d_branch[...] = (base_ref[...] * ls_ref[...]).astype(BF16)

    grad_in, grad_proj = [], []
    for chunk in range(3):
        hidden = slice(256 * chunk, 256 * chunk + 256)
        pre = dot(normed[...], we_ref[:, hidden]) + be_ref[hidden][None, :]
        phi = 0.5 * (1.0 + lax.erf(pre * ROOT_HALF))
        act = (pre * phi).astype(BF16)
        slope = phi + pre * INV_ROOT_TAU * jnp.exp(-0.5 * pre * pre)
        d_act = dot(d_branch[...], wp_ref[:, hidden])
        d_pre = (d_act * slope).astype(BF16)
        forward = dot_tb(act, wp_ref[:, hidden])
        backward = dot_tb(d_pre, we_ref[:, hidden])
        if chunk == 0:
            branch[...] = forward
            d_normed[...] = backward
        else:
            branch[...] += forward
            d_normed[...] += backward
        grad_in.append(dot_ta(normed[...], d_pre) * SCALE)
        grad_proj.append(dot_ta(act, d_branch[...]) * SCALE)
    grad_in = jnp.concatenate(grad_in, axis=1)
    grad_proj = jnp.concatenate(grad_proj, axis=0)
    for half in range(2):
        for x in range(2):
            gi_ref[half, x] = jnp.concatenate(
                [grad_in[24 * d : 24 * d + 24] for d in (4 * x + half, 4 * x + 2 + half)], axis=0
            ).astype(BF16)
            gp_ref[half, x] = jnp.concatenate(
                [grad_proj[96 * d : 96 * d + 96] for d in (4 * x + half, 4 * x + 2 + half)], axis=1
            ).astype(BF16)


    pl.semaphore_wait(barrier, len(peers))
    core_copies = [
        remote(gi_ref.at[1 - core], core_i, core_send.at[0], core_recv.at[0], (other, me)),
        remote(gp_ref.at[1 - core], core_p, core_send.at[1], core_recv.at[1], (other, me)),
    ]
    for copy in core_copies:
        copy.start()

    for p, (left, right) in enumerate(zip(*[iter(columns_of(x_ref))] * 2)):
        pair = []
        for j, column in ((2 * p, left), (2 * p + 1, right)):
            value = (branch[j * TS : j * TS + TS, :] + bp_ref[...]).astype(BF16).astype(F32)
            pair.append(jnp.where(inside, column + ls_ref[...] * value, 0.0))
        out_ref[:, p * PAIR : (p + 1) * PAIR] = jnp.concatenate(pair, axis=1).astype(BF16)

    d_pad[...] = jnp.zeros_like(d_pad)

    @pl.loop(0, 6)
    def _(block):
        rows = pl.ds(pl.multiple_of(block * 96, 96), 96)
        grad = d_normed[rows, :].astype(BF16).astype(F32) * gain_ref[...]
        scaled = normal[rows, :]
        mean = jnp.mean(grad, axis=1, keepdims=True)
        along = jnp.mean(grad * scaled, axis=1, keepdims=True)
        value = rstd[rows, 0:1] * (grad - mean - scaled * along)
        for j in range(4):
            d_pad[block * 4 + j + 6, 8:32] = value[j * TS : j * TS + TS]

    for copy in core_copies:
        copy.wait()
    for x in range(2):
        sum_i = gi_ref[core, x].astype(F32) + core_i[x].astype(F32)
        sum_p = gp_ref[core, x].astype(F32) + core_p[x].astype(F32)
        own_x_i[x] = sum_i
        own_x_p[x] = sum_p
        xs_i[x] = sum_i.astype(BF16)
        xs_p[x] = sum_p.astype(BF16)

    def x_copy(n, x, wide):
        if wide:
            return remote(xs_i.at[x], xr_i.at[n], x_send.at[n], x_recv.at[n], at_x(x))
        return remote(xs_p.at[x - 2], xr_p.at[n], x_send.at[n], x_recv.at[n], at_x(x))

    for n, x in enumerate(xs):

        @pl.when(x < 2)
        def _():
            x_copy(n, x, True).start()

        @pl.when(x >= 2)
        def _():
            x_copy(n, x, False).start()

    @pl.loop(0, 36)
    def _(at):
        whole = d_pad[at]
        for a in range(7):
            d_at[a, at] = whole[8 - a : 40 - a]

    @pl.loop(0, 10)
    def _(block):
        first = block * 3
        totals = [jnp.zeros((32, C), F32) for _ in range(3)]
        for a in range(7):
            for column in range(9):
                value = d_at[a, first + column].reshape(4, 8, C)
                for j in range(3):
                    b = j - column + 6
                    if 0 <= b < 7:
                        totals[j] = totals[j] + (value * weights[7 * a + b][None]).reshape(32, C)
        for j in range(3):
            d_ext[first + j] = totals[j]

    parts = []
    j = iota((TS, 1), 0)
    for m in range(6):
        parts.append(j * 32 + ((2 - m // 2) if m % 2 == 0 else (tile_len + 3 + m // 2)))
    middle = d_ext[3:27].reshape(TS * 32, C).astype(BF16)
    edge_rows = dot(one_hot(iota((144, TS * 32), 1), jnp.concatenate(parts, axis=0)), middle)
    parts = []
    for k in range(3):
        parts += [
            edge_rows[48 * k : 48 * k + 48],
            d_ext[2 - k, 3:27],
            d_ext[27 + k, 3:27],
        ]
    dh_ref[...] = jnp.concatenate(parts, axis=0).astype(BF16)
    dh_copies = [
        remote(dh_ref, dh_lo, dh_send.at[0], dh_recv.at[0], (dp, hi)),
        remote(dh_ref, dh_hi, dh_send.at[1], dh_recv.at[1], (dp, lo)),
    ]
    for copy in dh_copies:
        copy.start()

    def regroup(wide):
        if wide:
            total = own_x_i[mx]
            for n in range(3):
                total = total + xr_i[n].astype(F32)
        else:
            total = own_x_p[mx - 2]
            for n in range(3):
                total = total + xr_p[n].astype(F32)
        total = total.astype(BF16)
        run = iota((24, 1), 0)
        height = 48 if wide else 96
        runs = None
        for part in range(8 if wide else 4):
            rows = []
            for y in range(4):
                for h in range(4):
                    if wide:
                        row = jnp.where(run % 8 == part, 24 * (y % 2) + 12 * (y // 2) + 3 * h + run // 8, -1)
                    elif part // 2 == y % 2:
                        row = jnp.where(run % 2 == part % 2, 48 * (y // 2) + 12 * h + run // 2, -1)
                    else:
                        row = jnp.full((24, 1), -1, jnp.int32)
                    rows.append(row)
            pick = one_hot(iota((384, height), 1), jnp.concatenate(rows, axis=0))
            term = dot(pick, total[:, 96 * part : 96 * part + 96])
            runs = term if runs is None else runs + term
        for y in range(4):
            at_y = [runs[96 * y + 24 * h : 96 * y + 24 * h + 24] for h in range(4)]
            y_send_buf[y] = jnp.concatenate(at_y, axis=1).astype(BF16)

    @pl.when(mx < 2)
    def _():
        for n, x in enumerate(xs):
            remote(xs_i.at[0], xr_i.at[n], x_send.at[n], x_recv.at[n], at_x(x)).wait_recv()
        regroup(True)

    @pl.when(mx >= 2)
    def _():
        for n, x in enumerate(xs):
            remote(xs_p.at[0], xr_p.at[n], x_send.at[n], x_recv.at[n], at_x(x)).wait_recv()
        regroup(False)

    y_copies = [
        remote(y_send_buf.at[y], y_recv_buf.at[n], y_send.at[n], y_recv.at[n], at_y(y))
        for n, y in enumerate(ys)
    ]
    for copy in y_copies:
        copy.start()

    for j in range(TS):
        base_ref[j * TS : j * TS + TS, :] += d_ext[3 + j, 3:27]


    spread = []
    lane = iota((1, 96), 1)
    for source in range(3):
        sender = lax.rem(me + source + TILES - 1, TILES)
        target = jnp.full((1, 96), -1, jnp.int32)
        for q in range(4):
            code = code_ref[q, sender]
            index, on_band = oriented(lane - TS * q, code, shift_ref[q, sender])
            first = jnp.where(step_ref[q, sender] == 1 - source, (code // 2) * TS, -1000)
            mine = (lane >= TS * q) & (lane < TS * q + TS)
            target = jnp.where(mine & on_band, first + index, target)
        spread.append(one_hot(iota((96, 96), 0), target))
    cell = jnp.concatenate(band_cells(tile_len), axis=0)
    to_bands = one_hot(iota((288, CELLS), 1), cell)
    for copy in y_copies:
        copy.wait()
    total = y_send_buf[my].astype(F32)
    for n in range(3):
        total = total + y_recv_buf[n].astype(F32)
    for h in range(4):
        for row in range(8):
            z_send_buf[8 * h + row] = total[3 * row : 3 * row + 3, 96 * h : 96 * h + 96].astype(BF16)
    z_copies = [
        remote(z_send_buf.at[other_z], z_recv_buf.at[n], z_send, z_recv, at_z(other_z))
        for n, other_z in enumerate(zs)
    ]
    for copy in z_copies:
        copy.start()

    for copy in dh_copies:
        copy.wait()
    parts = []
    for k in range(3):
        rows = slice(96 * k, 96 * k + 96)
        parts.append(
            dot(spread[0], dh_lo[rows, :])
            + dot(spread[1], dh_ref[rows, :])
            + dot(spread[2], dh_hi[rows, :])
        )
    d_bands = jnp.concatenate(parts, axis=0)
    upper = d_bands.astype(BF16)
    lower = (d_bands - upper.astype(F32)).astype(BF16)
    total = base_ref[...] + (dot_ta(to_bands, upper) + dot_ta(to_bands, lower))
    inside = iota((TS, PAIR), 0) < tile_len
    for p in range(TS // 2):
        pair = [total[j * TS : j * TS + TS] for j in (2 * p, 2 * p + 1)]
        ig_ref[:, p * PAIR : (p + 1) * PAIR] = jnp.where(
            inside, jnp.concatenate(pair, axis=1), 0.0
        ).astype(BF16)

    remote(z_recv_buf, z_recv_buf, z_send, z_recv, (other, me)).wait()
    total = z_send_buf[z].astype(F32)
    for n in range(31):
        total = total + z_recv_buf[n].astype(F32)
    wg_ref[...] = jnp.concatenate([total[t : t + 1] for t in range(3)], axis=1)

    for n, x in enumerate(xs):

        @pl.when(x < 2)
        def _():
            x_copy(n, x, True).wait_send()

        @pl.when(x >= 2)
        def _():
            x_copy(n, x, False).wait_send()


def local(
    inputs,
    cotangent,
    tile_rows,
    neighbour_step,
    neighbour_code,
    neighbour_shift,
    conv_kernel,
    conv_bias,
    norm_gain,
    norm_bias,
    w_expand,
    b_expand,
    w_project,
    b_project,
    layer_scale,
):
    x = inputs.reshape(TS, WIDE)
    c = cotangent.reshape(TS, WIDE)
    tables = (neighbour_step.T, neighbour_code.T, neighbour_shift.T)
    dma = pltpu.SemaphoreType.DMA
    halo = pl.pallas_call(
        bands_kernel,
        out_shape=jax.ShapeDtypeStruct((288, C), BF16),
        in_specs=[SMEM] * 4 + [VMEM],
        out_specs=VMEM,
        scratch_shapes=[pltpu.VMEM((288, C), BF16)] * 3 + [dma((2,)), dma((2,))],
        compiler_params=pltpu.CompilerParams(
            collective_id=0, has_side_effects=True, vmem_limit_bytes=16 << 20
        ),
        name="bands",
    )(tile_rows, *tables, x)
    vm = pltpu.VMEM
    out, ig, wg = pl.pallas_call(
        main_kernel,
        out_shape=(
            jax.ShapeDtypeStruct((TS, WIDE), BF16),
            jax.ShapeDtypeStruct((TS, WIDE), BF16),
            jax.ShapeDtypeStruct((1, 288), F32),
        ),
        in_specs=[SMEM] * 4 + [VMEM] * 12,
        out_specs=(VMEM,) * 3,
        scratch_shapes=[
            vm((49, 8, C), F32),
            vm((30, 40, C), F32),
            vm((7, 30, TS, C), F32),
            vm((CELLS, C), F32),
            vm((CELLS, C), F32),
            vm((CELLS, 128), F32),
            vm((CELLS, C), BF16),
            vm((CELLS, C), BF16),
            vm((CELLS, C), F32),
            vm((CELLS, C), F32),
            vm((36, 40, C), F32),
            vm((7, 36, 32, C), F32),
            vm((30, 32, C), F32),
            vm((CELLS, C), F32),
            vm((288, C), BF16),
            vm((2, 2, 48, H), BF16),
            vm((2, 2, 96, PAIR), BF16),
            vm((288, C), BF16),
            vm((288, C), BF16),
            vm((2, 48, H), BF16),
            vm((2, 96, PAIR), BF16),
            vm((2, 48, H), BF16),
            vm((2, 96, PAIR), BF16),
            vm((3, 48, H), BF16),
            vm((3, 96, PAIR), BF16),
            vm((2, 48, H), F32),
            vm((2, 96, PAIR), F32),
            vm((4, 24, PAIR), BF16),
            vm((3, 24, PAIR), BF16),
            vm((32, 3, 96), BF16),
            vm((31, 3, 96), BF16),
        ]
        + [dma((2,))] * 4
        + [dma((3,))] * 4
        + [dma] * 2,
        compiler_params=pltpu.CompilerParams(
            collective_id=1, has_side_effects=True, vmem_limit_bytes=52 << 20
        ),
        name="main",
    )(
        tile_rows,
        *tables,
        x,
        c,
        halo,
        conv_kernel,
        conv_bias.reshape(1, C),
        norm_gain.reshape(1, C),
        norm_bias.reshape(1, C),
        w_expand,
        b_expand,
        w_project.T,
        b_project.reshape(1, C),
        layer_scale.reshape(1, C),
    )
    return (
        out.reshape(1, 1, TS, WIDE),
        ig.reshape(1, 1, TS, WIDE),
        wg.reshape(288),
    )


def solution(mesh):
    field = P("dp", "space", None, None)
    return jax.shard_map(
        local,
        mesh=mesh,
        in_specs=(field, field) + (P(),) * 13,
        out_specs=(field, field, P(("dp", "space"))),
        check_vma=False,
    )
```

```python
import math

import jax
import jax.numpy as jnp
from jax import lax
from jax.experimental import pallas as pl
from jax.experimental.pallas import tpu as pltpu
from jax.sharding import PartitionSpec as P

C = 192
H = 768
TS = 24
CELLS = TS * TS
TILES = 64
SAMPLES = 16
WIDE = TS * C
PAIR = 2 * C
ROOT_HALF = 0.7071067811865476
INV_ROOT_TAU = 0.3989422804014327
SCALE = 1.0 / math.sqrt(SAMPLES * TILES * CELLS)
F32 = jnp.float32
BF16 = jnp.bfloat16
MESH = pl.DeviceIdType.MESH
SMEM = pl.BlockSpec(memory_space=pltpu.SMEM)
VMEM = pl.BlockSpec(memory_space=pltpu.VMEM)
ANY = pl.BlockSpec(memory_space=pl.ANY)
BUDGET = 58 << 20


def iota(shape, dim):
    return lax.broadcasted_iota(jnp.int32, shape, dim)


def one_hot(found, wanted):
    return jnp.where(found == wanted, 1.0, 0.0).astype(BF16)


def dot(a, b):
    return jnp.dot(a, b, preferred_element_type=F32)


def dot_tb(a, b):
    return lax.dot_general(a, b, (((1,), (1,)), ((), ())), preferred_element_type=F32)


def dot_ta(a, b):
    return lax.dot_general(a, b, (((0,), (0,)), ((), ())), preferred_element_type=F32)


def columns_of(ref):
    columns = []
    for p in range(TS // 2):
        pair = ref[:, p * PAIR : (p + 1) * PAIR].astype(F32)
        columns += [pair[:, :C], pair[:, C:]]
    return columns


def packed(rows):
    return jnp.concatenate([rows[:144], rows[144:]], axis=1).astype(BF16)


def unpacked(ref):
    both = ref[...].astype(F32)
    return jnp.concatenate([both[:, :C], both[:, C:]], axis=0).astype(BF16)


def band_cells(tile_len):
    i = iota((TS, 1), 0)
    parts = []
    for k in range(3):
        parts.append(i * TS + k)
        parts.append(i * TS + (tile_len - 1 - k))
        parts.append(jnp.where(i < tile_len, k * TS + i, -1))
        parts.append(jnp.where(i < tile_len, (TS - 1 - k) * TS + i, -1))
    return parts


def oriented(position, code, shift):
    unshifted = position - shift
    index = jnp.where(code % 2 == 1, TS - 1 - unshifted, unshifted)
    return index, (unshifted >= 0) & (unshifted < TS)


def bands_kernel(
    rows_ref,
    step_ref,
    code_ref,
    shift_ref,
    x_hbm,
    halo_ref,
    x_ref,
    own,
    from_lo,
    from_hi,
    load,
    send,
    recv,
):
    load_x = pltpu.make_async_copy(x_hbm, x_ref, load)
    load_x.start()
    me = lax.axis_index("space")
    dp = lax.axis_index("dp")
    hi = lax.rem(me + 1, TILES)
    lo = lax.rem(me + TILES - 1, TILES)
    barrier = pltpu.get_barrier_semaphore()
    for peer in (lo, hi):
        pl.semaphore_signal(barrier, inc=1, device_id=(dp, peer), device_id_type=MESH)
    wanted = jnp.concatenate(band_cells(rows_ref[me]), axis=0)
    pick = one_hot(iota((288, CELLS), 1), wanted)
    load_x.wait()
    cells = jnp.concatenate(columns_of(x_ref), axis=0).astype(BF16)
    bands = dot(pick, cells)
    own[...] = packed(bands)
    bands = bands.astype(BF16)
    pl.semaphore_wait(barrier, 2)
    copies = []
    for n, (peer, landing) in enumerate(((hi, from_lo), (lo, from_hi))):
        copy = pltpu.make_async_remote_copy(
            src_ref=own,
            dst_ref=landing,
            send_sem=send.at[n],
            recv_sem=recv.at[n],
            device_id=(dp, peer),
            device_id_type=MESH,
        )
        copy.start()
        copies.append(copy)
    position = iota((TS, 1), 0)
    picks = []
    for source in range(3):
        parts = []
        for q in range(4):
            code = code_ref[q, me]
            index, on_band = oriented(position, code, shift_ref[q, me])
            first = jnp.where(step_ref[q, me] + 1 == source, (code // 2) * TS, -1000)
            parts.append(jnp.where(on_band, first + index, -1))
        picks.append(one_hot(iota((96, 96), 1), jnp.concatenate(parts, axis=0)))
    for copy in copies:
        copy.wait()
    below, above = unpacked(from_lo), unpacked(from_hi)
    for k in range(3):
        rows = slice(96 * k, 96 * k + 96)
        halo_ref[rows, :] = (
            dot(picks[0], below[rows]) + dot(picks[1], bands[rows]) + dot(picks[2], above[rows])
        ).astype(BF16)


def main_kernel(
    rows_ref,
    step_ref,
    code_ref,
    shift_ref,
    x_hbm,
    c_hbm,
    halo_ref,
    kern_ref,
    bias_ref,
    gain_ref,
    nbias_ref,
    we_hbm,
    be_ref,
    wp_hbm,
    bp_ref,
    ls_ref,
    out_ref,
    ig_ref,
    wg_ref,
    x_ref,
    c_ref,
    we_ref,
    wp_ref,
    load,
    weights,
    ext,
    ext_at,
    mixed,
    normal,
    rstd,
    normed,
    d_branch,
    branch,
    d_normed,
    d_pad,
    d_at,
    d_ext,
    base_ref,
    dh_ref,
    gi_ref,
    gp_ref,
    dh_lo,
    dh_hi,
    core_i,
    core_p,
    xs_i,
    xs_p,
    xr_i,
    xr_p,
    own_x_i,
    own_x_p,
    y_send_buf,
    y_recv_buf,
    z_send_buf,
    z_recv_buf,
    dh_send,
    dh_recv,
    core_send,
    core_recv,
    x_send,
    x_recv,
    y_send,
    y_recv,
    z_send,
    z_recv,
):
    loads = [
        pltpu.make_async_copy(source, landing, load.at[n])
        for n, (source, landing) in enumerate(
            ((x_hbm, x_ref), (c_hbm, c_ref), (we_hbm, we_ref), (wp_hbm, wp_ref))
        )
    ]
    for copy in loads:
        copy.start()
    me = lax.axis_index("space")
    dp = lax.axis_index("dp")
    mx = dp // 4
    core = lax.rem(dp, 2)
    my = (me // 32) * 2 + lax.rem(dp // 2, 2)
    z = lax.rem(me, 32)
    hi = lax.rem(me + 1, TILES)
    lo = lax.rem(me + TILES - 1, TILES)
    other = dp + 1 - 2 * core

    def at_x(x):
        return (x * 4 + lax.rem(dp, 4), me)

    def at_y(y):
        return (mx * 4 + lax.rem(y, 2) * 2 + core, (y // 2) * 32 + z)

    def at_z(other_z):
        return (dp, me - z + other_z)

    xs = [lax.rem(mx + d, 4) for d in (1, 2, 3)]
    ys = [lax.rem(my + d, 4) for d in (1, 2, 3)]
    far_first = sorted(range(1, 32), key=lambda d: -min(d, 32 - d))
    zs = [lax.rem(z + d, 32) for d in far_first]
    peers = [at_z(other_z) for other_z in zs] + [at_y(y) for y in ys] + [at_x(x) for x in xs]
    peers += [(dp, lo), (dp, hi), (other, me)]
    barrier = pltpu.get_barrier_semaphore()
    for peer in peers:
        pl.semaphore_signal(barrier, inc=1, device_id=peer, device_id_type=MESH)

    def remote(source, landing, send, recv, peer):
        return pltpu.make_async_remote_copy(
            src_ref=source,
            dst_ref=landing,
            send_sem=send,
            recv_sem=recv,
            device_id=peer,
            device_id_type=MESH,
        )

    tile_len = rows_ref[me]
    inside = iota((TS, C), 0) < tile_len
    for t in range(49):
        weights[t] = jnp.broadcast_to(kern_ref[t // 7, t % 7 : t % 7 + 1, :], (8, C))

    halo = halo_ref[...].astype(F32)
    col = iota((1, 144), 1)
    target = col
    for m in range(6):
        row = (7 - m // 2) if m % 2 == 0 else (tile_len + 8 + m // 2)
        target = jnp.where(col >= TS * m, col * 40 + (row - 960 * m), target)
    edge_rows = jnp.concatenate([halo[96 * k : 96 * k + 48] for k in range(3)], axis=0).astype(BF16)
    ext[3:27] = dot(one_hot(iota((960, 144), 0), target), edge_rows).reshape(TS, 40, C)
    blank = jnp.zeros((40, C), F32)
    for k in range(3):
        ext[2 - k] = blank
        ext[27 + k] = blank
        ext[2 - k, 8:32] = halo[96 * k + 48 : 96 * k + 72]
        ext[27 + k, 8:32] = halo[96 * k + 72 : 96 * k + 96]
    loads[0].wait()
    for j, column in enumerate(columns_of(x_ref)):
        ext[3 + j, 8:32] += jnp.where(inside, column, 0.0)

    @pl.loop(0, 30)
    def _(at):
        whole = ext[at]
        for a in range(7):
            ext_at[a, at] = whole[5 + a : 29 + a]

    @pl.loop(0, 6)
    def _(block):
        first = block * 4
        totals = [jnp.broadcast_to(bias_ref[...], (TS, C)) for _ in range(4)]
        for a in range(7):
            for column in range(10):
                value = ext_at[a, first + column].reshape(3, 8, C)
                for j in range(4):
                    b = column - j
                    if 0 <= b < 7:
                        totals[j] = totals[j] + (value * weights[7 * a + b][None]).reshape(TS, C)
        for j in range(4):
            mixed[pl.ds((first + j) * TS, TS), :] = totals[j]

    @pl.loop(0, 6)
    def _(block):
        rows = pl.ds(pl.multiple_of(block * 96, 96), 96)
        value = mixed[rows, :]
        centred = value - jnp.mean(value, axis=1, keepdims=True)
        inverse = lax.rsqrt(jnp.mean(centred * centred, axis=1, keepdims=True) + 1e-06)
        scaled = centred * inverse
        normal[rows, :] = scaled
        rstd[rows, :] = jnp.broadcast_to(inverse, (96, 128))
        normed[rows, :] = (scaled * gain_ref[...] + nbias_ref[...]).astype(BF16)

    for copy in loads[1:]:
        copy.wait()
    grads = [jnp.where(inside, column, 0.0) for column in columns_of(c_ref)]
    for j in range(TS):
        base_ref[j * TS : j * TS + TS, :] = grads[j]
    d_branch[...] = (base_ref[...] * ls_ref[...]).astype(BF16)

    grad_in, grad_proj = [], []
    for chunk in range(3):
        hidden = slice(256 * chunk, 256 * chunk + 256)
        pre = dot(normed[...], we_ref[:, hidden]) + be_ref[hidden][None, :]
        phi = 0.5 * (1.0 + lax.erf(pre * ROOT_HALF))
        act = (pre * phi).astype(BF16)
        slope = phi + pre * INV_ROOT_TAU * jnp.exp(-0.5 * pre * pre)
        d_act = dot(d_branch[...], wp_ref[:, hidden])
        d_pre = (d_act * slope).astype(BF16)
        forward = dot_tb(act, wp_ref[:, hidden])
        backward = dot_tb(d_pre, we_ref[:, hidden])
        if chunk == 0:
            branch[...] = forward
            d_normed[...] = backward
        else:
            branch[...] += forward
            d_normed[...] += backward
        grad_in.append(dot_ta(normed[...], d_pre) * SCALE)
        grad_proj.append(dot_ta(act, d_branch[...]) * SCALE)
    grad_in = jnp.concatenate(grad_in, axis=1)
    grad_proj = jnp.concatenate(grad_proj, axis=0)
    for half in range(2):
        for x in range(2):
            gi_ref[half, x] = jnp.concatenate(
                [grad_in[24 * d : 24 * d + 24] for d in (4 * x + half, 4 * x + 2 + half)], axis=0
            ).astype(BF16)
            gp_ref[half, x] = jnp.concatenate(
                [grad_proj[96 * d : 96 * d + 96] for d in (4 * x + half, 4 * x + 2 + half)], axis=1
            ).astype(BF16)


    pl.semaphore_wait(barrier, len(peers))
    core_copies = [
        remote(gi_ref.at[1 - core], core_i, core_send.at[0], core_recv.at[0], (other, me)),
        remote(gp_ref.at[1 - core], core_p, core_send.at[1], core_recv.at[1], (other, me)),
    ]
    for copy in core_copies:
        copy.start()

    for p, (left, right) in enumerate(zip(*[iter(columns_of(x_ref))] * 2)):
        pair = []
        for j, column in ((2 * p, left), (2 * p + 1, right)):
            value = (branch[j * TS : j * TS + TS, :] + bp_ref[...]).astype(BF16).astype(F32)
            pair.append(jnp.where(inside, column + ls_ref[...] * value, 0.0))
        out_ref[:, p * PAIR : (p + 1) * PAIR] = jnp.concatenate(pair, axis=1).astype(BF16)

    d_pad[...] = jnp.zeros_like(d_pad)

    @pl.loop(0, 6)
    def _(block):
        rows = pl.ds(pl.multiple_of(block * 96, 96), 96)
        grad = d_normed[rows, :].astype(BF16).astype(F32) * gain_ref[...]
        scaled = normal[rows, :]
        mean = jnp.mean(grad, axis=1, keepdims=True)
        along = jnp.mean(grad * scaled, axis=1, keepdims=True)
        value = rstd[rows, 0:1] * (grad - mean - scaled * along)
        for j in range(4):
            d_pad[block * 4 + j + 6, 8:32] = value[j * TS : j * TS + TS]

    for copy in core_copies:
        copy.wait()
    for x in range(2):
        sum_i = gi_ref[core, x].astype(F32) + core_i[x].astype(F32)
        sum_p = gp_ref[core, x].astype(F32) + core_p[x].astype(F32)
        own_x_i[x] = sum_i
        own_x_p[x] = sum_p
        xs_i[x] = sum_i.astype(BF16)
        xs_p[x] = sum_p.astype(BF16)

    def x_copy(n, x, wide):
        if wide:
            return remote(xs_i.at[x], xr_i.at[n], x_send.at[n], x_recv.at[n], at_x(x))
        return remote(xs_p.at[x - 2], xr_p.at[n], x_send.at[n], x_recv.at[n], at_x(x))

    for n, x in enumerate(xs):

        @pl.when(x < 2)
        def _():
            x_copy(n, x, True).start()

        @pl.when(x >= 2)
        def _():
            x_copy(n, x, False).start()

    @pl.loop(0, 36)
    def _(at):
        whole = d_pad[at]
        for a in range(7):
            d_at[a, at] = whole[8 - a : 40 - a]

    @pl.loop(0, 10)
    def _(block):
        first = block * 3
        totals = [jnp.zeros((32, C), F32) for _ in range(3)]
        for a in range(7):
            for column in range(9):
                value = d_at[a, first + column].reshape(4, 8, C)
                for j in range(3):
                    b = j - column + 6
                    if 0 <= b < 7:
                        totals[j] = totals[j] + (value * weights[7 * a + b][None]).reshape(32, C)
        for j in range(3):
            d_ext[first + j] = totals[j]

    parts = []
    j = iota((TS, 1), 0)
    for m in range(6):
        parts.append(j * 32 + ((2 - m // 2) if m % 2 == 0 else (tile_len + 3 + m // 2)))
    middle = d_ext[3:27].reshape(TS * 32, C).astype(BF16)
    edge_rows = dot(one_hot(iota((144, TS * 32), 1), jnp.concatenate(parts, axis=0)), middle)
    parts = []
    for k in range(3):
        parts += [
            edge_rows[48 * k : 48 * k + 48],
            d_ext[2 - k, 3:27],
            d_ext[27 + k, 3:27],
        ]
    own_dh = jnp.concatenate(parts, axis=0)
    dh_ref[...] = packed(own_dh)
    own_dh = own_dh.astype(BF16)
    dh_copies = [
        remote(dh_ref, dh_lo, dh_send.at[0], dh_recv.at[0], (dp, hi)),
        remote(dh_ref, dh_hi, dh_send.at[1], dh_recv.at[1], (dp, lo)),
    ]
    for copy in dh_copies:
        copy.start()

    def regroup(wide):
        if wide:
            total = own_x_i[mx]
            for n in range(3):
                total = total + xr_i[n].astype(F32)
        else:
            total = own_x_p[mx - 2]
            for n in range(3):
                total = total + xr_p[n].astype(F32)
        total = total.astype(BF16)
        run = iota((24, 1), 0)
        height = 48 if wide else 96
        runs = None
        for part in range(8 if wide else 4):
            rows = []
            for y in range(4):
                for h in range(4):
                    if wide:
                        row = jnp.where(run % 8 == part, 24 * (y % 2) + 12 * (y // 2) + 3 * h + run // 8, -1)
                    elif part // 2 == y % 2:
                        row = jnp.where(run % 2 == part % 2, 48 * (y // 2) + 12 * h + run // 2, -1)
                    else:
                        row = jnp.full((24, 1), -1, jnp.int32)
                    rows.append(row)
            pick = one_hot(iota((384, height), 1), jnp.concatenate(rows, axis=0))
            term = dot(pick, total[:, 96 * part : 96 * part + 96])
            runs = term if runs is None else runs + term
        for y in range(4):
            at_y = [runs[96 * y + 24 * h : 96 * y + 24 * h + 24] for h in range(4)]
            y_send_buf[y] = jnp.concatenate(at_y, axis=1).astype(BF16)

    @pl.when(mx < 2)
    def _():
        for n, x in enumerate(xs):
            remote(xs_i.at[0], xr_i.at[n], x_send.at[n], x_recv.at[n], at_x(x)).wait_recv()
        regroup(True)

    @pl.when(mx >= 2)
    def _():
        for n, x in enumerate(xs):
            remote(xs_p.at[0], xr_p.at[n], x_send.at[n], x_recv.at[n], at_x(x)).wait_recv()
        regroup(False)

    y_copies = [
        remote(y_send_buf.at[y], y_recv_buf.at[n], y_send.at[n], y_recv.at[n], at_y(y))
        for n, y in enumerate(ys)
    ]
    for copy in y_copies:
        copy.start()

    for j in range(TS):
        base_ref[j * TS : j * TS + TS, :] += d_ext[3 + j, 3:27]


    spread = []
    lane = iota((1, 96), 1)
    for source in range(3):
        sender = lax.rem(me + source + TILES - 1, TILES)
        target = jnp.full((1, 96), -1, jnp.int32)
        for q in range(4):
            code = code_ref[q, sender]
            index, on_band = oriented(lane - TS * q, code, shift_ref[q, sender])
            first = jnp.where(step_ref[q, sender] == 1 - source, (code // 2) * TS, -1000)
            mine = (lane >= TS * q) & (lane < TS * q + TS)
            target = jnp.where(mine & on_band, first + index, target)
        spread.append(one_hot(iota((96, 96), 0), target))
    cell = jnp.concatenate(band_cells(tile_len), axis=0)
    to_bands = one_hot(iota((288, CELLS), 1), cell)
    for copy in y_copies:
        copy.wait()
    total = y_send_buf[my].astype(F32)
    for n in range(3):
        total = total + y_recv_buf[n].astype(F32)
    for h in range(4):
        for row in range(8):
            z_send_buf[8 * h + row] = total[3 * row : 3 * row + 3, 96 * h : 96 * h + 96].astype(BF16)
    z_copies = [
        remote(z_send_buf.at[other_z], z_recv_buf.at[n], z_send, z_recv, at_z(other_z))
        for n, other_z in enumerate(zs)
    ]
    for copy in z_copies:
        copy.start()

    for copy in dh_copies:
        copy.wait()
    below, above = unpacked(dh_lo), unpacked(dh_hi)
    parts = []
    for k in range(3):
        rows = slice(96 * k, 96 * k + 96)
        parts.append(
            dot(spread[0], below[rows]) + dot(spread[1], own_dh[rows]) + dot(spread[2], above[rows])
        )
    d_bands = jnp.concatenate(parts, axis=0)
    upper = d_bands.astype(BF16)
    lower = (d_bands - upper.astype(F32)).astype(BF16)
    total = base_ref[...] + (dot_ta(to_bands, upper) + dot_ta(to_bands, lower))
    inside = iota((TS, PAIR), 0) < tile_len
    for p in range(TS // 2):
        pair = [total[j * TS : j * TS + TS] for j in (2 * p, 2 * p + 1)]
        ig_ref[:, p * PAIR : (p + 1) * PAIR] = jnp.where(
            inside, jnp.concatenate(pair, axis=1), 0.0
        ).astype(BF16)

    remote(z_recv_buf, z_recv_buf, z_send, z_recv, (other, me)).wait()
    total = z_send_buf[z].astype(F32)
    for n in range(31):
        total = total + z_recv_buf[n].astype(F32)
    wg_ref[...] = jnp.concatenate([total[t : t + 1] for t in range(3)], axis=1)

    for n, x in enumerate(xs):

        @pl.when(x < 2)
        def _():
            x_copy(n, x, True).wait_send()

        @pl.when(x >= 2)
        def _():
            x_copy(n, x, False).wait_send()


def emit_kernel(out_ref, ig_ref, wg_ref, out_hbm, ig_hbm, wg_hbm, sems):
    pairs = ((out_ref, out_hbm), (ig_ref, ig_hbm), (wg_ref.at[0], wg_hbm))
    copies = [
        pltpu.make_async_copy(source, landing, sems.at[n])
        for n, (source, landing) in enumerate(pairs)
    ]
    for copy in copies:
        copy.start()
    for copy in copies:
        copy.wait()


def local(
    inputs,
    cotangent,
    tile_rows,
    neighbour_step,
    neighbour_code,
    neighbour_shift,
    conv_kernel,
    conv_bias,
    norm_gain,
    norm_bias,
    w_expand,
    b_expand,
    w_project,
    b_project,
    layer_scale,
):
    x = inputs.reshape(TS, WIDE)
    c = cotangent.reshape(TS, WIDE)
    tables = (neighbour_step.T, neighbour_code.T, neighbour_shift.T)
    dma = pltpu.SemaphoreType.DMA
    halo = pl.pallas_call(
        bands_kernel,
        out_shape=jax.ShapeDtypeStruct((288, C), BF16),
        in_specs=[SMEM] * 4 + [ANY],
        out_specs=VMEM,
        scratch_shapes=[pltpu.VMEM((TS, WIDE), BF16)]
        + [pltpu.VMEM((144, PAIR), BF16)] * 3
        + [dma, dma((2,)), dma((2,))],
        compiler_params=pltpu.CompilerParams(
            collective_id=0, has_side_effects=True, vmem_limit_bytes=BUDGET
        ),
        name="bands",
    )(tile_rows, *tables, x)
    vm = pltpu.VMEM
    out, ig, wg = pl.pallas_call(
        main_kernel,
        out_shape=(
            jax.ShapeDtypeStruct((TS, WIDE), BF16),
            jax.ShapeDtypeStruct((TS, WIDE), BF16),
            jax.ShapeDtypeStruct((1, 288), F32),
        ),
        in_specs=[SMEM] * 4
        + [ANY, ANY]
        + [VMEM] * 5
        + [ANY, VMEM, ANY, VMEM, VMEM],
        out_specs=(VMEM,) * 3,
        scratch_shapes=[
            vm((TS, WIDE), BF16),
            vm((TS, WIDE), BF16),
            vm((C, H), BF16),
            vm((C, H), BF16),
            dma((4,)),
            vm((49, 8, C), F32),
            vm((30, 40, C), F32),
            vm((7, 30, TS, C), F32),
            vm((CELLS, C), F32),
            vm((CELLS, C), F32),
            vm((CELLS, 128), F32),
            vm((CELLS, C), BF16),
            vm((CELLS, C), BF16),
            vm((CELLS, C), F32),
            vm((CELLS, C), F32),
            vm((36, 40, C), F32),
            vm((7, 36, 32, C), F32),
            vm((30, 32, C), F32),
            vm((CELLS, C), F32),
            vm((144, PAIR), BF16),
            vm((2, 2, 48, H), BF16),
            vm((2, 2, 96, PAIR), BF16),
            vm((144, PAIR), BF16),
            vm((144, PAIR), BF16),
            vm((2, 48, H), BF16),
            vm((2, 96, PAIR), BF16),
            vm((2, 48, H), BF16),
            vm((2, 96, PAIR), BF16),
            vm((3, 48, H), BF16),
            vm((3, 96, PAIR), BF16),
            vm((2, 48, H), F32),
            vm((2, 96, PAIR), F32),
            vm((4, 24, PAIR), BF16),
            vm((3, 24, PAIR), BF16),
            vm((32, 3, 96), BF16),
            vm((31, 3, 96), BF16),
        ]
        + [dma((2,))] * 4
        + [dma((3,))] * 4
        + [dma] * 2,
        compiler_params=pltpu.CompilerParams(
            collective_id=1, has_side_effects=True, vmem_limit_bytes=BUDGET
        ),
        name="main",
    )(
        tile_rows,
        *tables,
        x,
        c,
        halo,
        conv_kernel,
        conv_bias.reshape(1, C),
        norm_gain.reshape(1, C),
        norm_bias.reshape(1, C),
        w_expand,
        b_expand,
        w_project.T,
        b_project.reshape(1, C),
        layer_scale.reshape(1, C),
    )
    out, ig, wg = pl.pallas_call(
        emit_kernel,
        out_shape=(
            jax.ShapeDtypeStruct((TS, WIDE), BF16),
            jax.ShapeDtypeStruct((TS, WIDE), BF16),
            jax.ShapeDtypeStruct((288,), F32),
        ),
        in_specs=[VMEM] * 3,
        out_specs=(ANY,) * 3,
        scratch_shapes=[dma((3,))],
        name="emit",
    )(out, ig, wg)
    return out.reshape(1, 1, TS, WIDE), ig.reshape(1, 1, TS, WIDE), wg


def solution(mesh):
    field = P("dp", "space", None, None)
    return jax.shard_map(
        local,
        mesh=mesh,
        in_specs=(field, field) + (P(),) * 13,
        out_specs=(field, field, P(("dp", "space"))),
        check_vma=False,
    )
```

```python
import math

import jax
import jax.numpy as jnp
from jax import lax
from jax.experimental import pallas as pl
from jax.experimental.pallas import tpu as pltpu
from jax.sharding import PartitionSpec as P

C = 192
H = 768
TS = 24
CELLS = TS * TS
TILES = 64
SAMPLES = 16
WIDE = TS * C
PAIR = 2 * C
ROOT_HALF = 0.7071067811865476
INV_ROOT_TAU = 0.3989422804014327
SCALE = 1.0 / math.sqrt(SAMPLES * TILES * CELLS)
F32 = jnp.float32
BF16 = jnp.bfloat16
MESH = pl.DeviceIdType.MESH
SMEM = pl.BlockSpec(memory_space=pltpu.SMEM)
VMEM = pl.BlockSpec(memory_space=pltpu.VMEM)
ANY = pl.BlockSpec(memory_space=pl.ANY)
BUDGET = 58 << 20


def iota(shape, dim):
    return lax.broadcasted_iota(jnp.int32, shape, dim)


def one_hot(found, wanted):
    return jnp.where(found == wanted, 1.0, 0.0).astype(BF16)


def dot(a, b):
    return jnp.dot(a, b, preferred_element_type=F32)


def dot_tb(a, b):
    return lax.dot_general(a, b, (((1,), (1,)), ((), ())), preferred_element_type=F32)


def dot_ta(a, b):
    return lax.dot_general(a, b, (((0,), (0,)), ((), ())), preferred_element_type=F32)


def columns_of(ref):
    columns = []
    for p in range(TS // 2):
        pair = ref[:, p * PAIR : (p + 1) * PAIR].astype(F32)
        columns += [pair[:, :C], pair[:, C:]]
    return columns


def packed(rows):
    return jnp.concatenate([rows[:144], rows[144:]], axis=1).astype(BF16)


def unpacked(ref):
    both = ref[...].astype(F32)
    return jnp.concatenate([both[:, :C], both[:, C:]], axis=0).astype(BF16)


def band_cells(tile_len):
    i = iota((TS, 1), 0)
    parts = []
    for k in range(3):
        parts.append(i * TS + k)
        parts.append(i * TS + (tile_len - 1 - k))
        parts.append(jnp.where(i < tile_len, k * TS + i, -1))
        parts.append(jnp.where(i < tile_len, (TS - 1 - k) * TS + i, -1))
    return parts


def oriented(position, code, shift):
    unshifted = position - shift
    index = jnp.where(code % 2 == 1, TS - 1 - unshifted, unshifted)
    return index, (unshifted >= 0) & (unshifted < TS)


def bands_kernel(
    rows_ref,
    step_ref,
    code_ref,
    shift_ref,
    x_hbm,
    kern_ref,
    bias_ref,
    halo_ref,
    mixed_ref,
    weights,
    ext_at,
    x_ref,
    own,
    from_lo,
    from_hi,
    load,
    send,
    recv,
):
    load_x = pltpu.make_async_copy(x_hbm, x_ref, load)
    load_x.start()
    me = lax.axis_index("space")
    dp = lax.axis_index("dp")
    hi = lax.rem(me + 1, TILES)
    lo = lax.rem(me + TILES - 1, TILES)
    barrier = pltpu.get_barrier_semaphore()
    for peer in (lo, hi):
        pl.semaphore_signal(barrier, inc=1, device_id=(dp, peer), device_id_type=MESH)
    wanted = jnp.concatenate(band_cells(rows_ref[me]), axis=0)
    pick = one_hot(iota((288, CELLS), 1), wanted)
    load_x.wait()
    cells = jnp.concatenate(columns_of(x_ref), axis=0).astype(BF16)
    bands = dot(pick, cells)
    own[...] = packed(bands)
    bands = bands.astype(BF16)
    pl.semaphore_wait(barrier, 2)
    copies = []
    for n, (peer, landing) in enumerate(((hi, from_lo), (lo, from_hi))):
        copy = pltpu.make_async_remote_copy(
            src_ref=own,
            dst_ref=landing,
            send_sem=send.at[n],
            recv_sem=recv.at[n],
            device_id=(dp, peer),
            device_id_type=MESH,
        )
        copy.start()
        copies.append(copy)
    position = iota((TS, 1), 0)
    picks = []
    for source in range(3):
        parts = []
        for q in range(4):
            code = code_ref[q, me]
            index, on_band = oriented(position, code, shift_ref[q, me])
            first = jnp.where(step_ref[q, me] + 1 == source, (code // 2) * TS, -1000)
            parts.append(jnp.where(on_band, first + index, -1))
        picks.append(one_hot(iota((96, 96), 1), jnp.concatenate(parts, axis=0)))
    tile_len = rows_ref[me]
    inside = iota((TS, C), 0) < tile_len
    for t in range(49):
        weights[t] = jnp.broadcast_to(kern_ref[t // 7, t % 7 : t % 7 + 1, :], (8, C))
    blank = jnp.zeros((7, TS, C), F32)
    for k in range(3):
        ext_at[:, k] = blank
        ext_at[:, 27 + k] = blank
    for j, column in enumerate(columns_of(x_ref)):
        whole = jnp.concatenate(
            [blank[0, :8], jnp.where(inside, column, 0.0), blank[0, :8]], axis=0
        )
        for a in range(7):
            ext_at[a, 3 + j] = whole[5 + a : 29 + a]

    @pl.loop(0, 6)
    def _(block):
        first = block * 4
        totals = [jnp.broadcast_to(bias_ref[...], (TS, C)) for _ in range(4)]
        for a in range(7):
            for column in range(10):
                value = ext_at[a, first + column].reshape(3, 8, C)
                for j in range(4):
                    b = column - j
                    if 0 <= b < 7:
                        totals[j] = totals[j] + (value * weights[7 * a + b][None]).reshape(TS, C)
        for j in range(4):
            at = pl.multiple_of((first + j) * TS, TS)
            mixed_ref[pl.ds(at, TS), :] = totals[j]

    for copy in copies:
        copy.wait()
    below, above = unpacked(from_lo), unpacked(from_hi)
    for k in range(3):
        rows = slice(96 * k, 96 * k + 96)
        halo_ref[rows, :] = (
            dot(picks[0], below[rows]) + dot(picks[1], bands[rows]) + dot(picks[2], above[rows])
        ).astype(BF16)


def main_kernel(
    rows_ref,
    step_ref,
    code_ref,
    shift_ref,
    x_hbm,
    c_hbm,
    halo_ref,
    field_mixed,
    kern_ref,
    gain_ref,
    nbias_ref,
    we_hbm,
    be_ref,
    wp_hbm,
    bp_ref,
    ls_ref,
    out_ref,
    ig_ref,
    wg_ref,
    x_ref,
    c_ref,
    we_ref,
    wp_ref,
    load,
    weights,
    mixed,
    normal,
    rstd,
    normed,
    d_branch,
    branch,
    d_normed,
    d_pad,
    d_at,
    d_ext,
    base_ref,
    dh_ref,
    gi_ref,
    gp_ref,
    dh_lo,
    dh_hi,
    core_i,
    core_p,
    xs_i,
    xs_p,
    xr_i,
    xr_p,
    own_x_i,
    own_x_p,
    y_send_buf,
    y_recv_buf,
    z_send_buf,
    z_recv_buf,
    dh_send,
    dh_recv,
    core_send,
    core_recv,
    x_send,
    x_recv,
    y_send,
    y_recv,
    z_send,
    z_recv,
    near_sem,
    far_sem,
):
    loads = [
        pltpu.make_async_copy(source, landing, load.at[n])
        for n, (source, landing) in enumerate(
            ((x_hbm, x_ref), (c_hbm, c_ref), (we_hbm, we_ref), (wp_hbm, wp_ref))
        )
    ]
    for copy in loads:
        copy.start()
    me = lax.axis_index("space")
    dp = lax.axis_index("dp")
    mx = dp // 4
    core = lax.rem(dp, 2)
    my = (me // 32) * 2 + lax.rem(dp // 2, 2)
    z = lax.rem(me, 32)
    hi = lax.rem(me + 1, TILES)
    lo = lax.rem(me + TILES - 1, TILES)
    other = dp + 1 - 2 * core

    def at_x(x):
        return (x * 4 + lax.rem(dp, 4), me)

    def at_y(y):
        return (mx * 4 + lax.rem(y, 2) * 2 + core, (y // 2) * 32 + z)

    def at_z(other_z):
        return (dp, me - z + other_z)

    xs = [lax.rem(mx + d, 4) for d in (1, 2, 3)]
    ys = [lax.rem(my + d, 4) for d in (1, 2, 3)]
    far_first = sorted(range(1, 32), key=lambda d: -min(d, 32 - d))
    zs = [lax.rem(z + d, 32) for d in far_first]
    near = [at_z(lax.rem(z + d, 32)) for d in (4, 28, 3, 29, 2, 30, 1, 31)]
    far = [at_z(lax.rem(z + d, 32)) for d in (8, 24)]
    peers = near + [at_y(y) for y in ys] + [at_x(x) for x in xs]
    peers += [(dp, lo), (dp, hi), (other, me)]
    barrier = pltpu.get_barrier_semaphore()
    for peer in peers:
        pl.semaphore_signal(barrier, inc=1, device_id=peer, device_id_type=MESH)

    def remote(source, landing, send, recv, peer):
        return pltpu.make_async_remote_copy(
            src_ref=source,
            dst_ref=landing,
            send_sem=send,
            recv_sem=recv,
            device_id=peer,
            device_id_type=MESH,
        )

    tile_len = rows_ref[me]
    inside = iota((TS, C), 0) < tile_len
    for t in range(49):
        weights[t] = jnp.broadcast_to(kern_ref[t // 7, t % 7 : t % 7 + 1, :], (8, C))

    halo = halo_ref[...].astype(F32)
    blank = jnp.zeros((8, C), F32)

    def framed(first):
        return jnp.concatenate([blank, halo[first : first + TS], blank], axis=0)

    sides = []
    for q in (2, 3):
        totals = [jnp.zeros((TS, C), F32) for _ in range(3)]
        for k in range(3):
            whole = framed(96 * k + TS * q)
            at = 2 - k if q == 2 else 27 + k
            for a in range(7):
                value = whole[5 + a : 29 + a].reshape(3, 8, C)
                for n in range(3):
                    b = at - (n if q == 2 else 21 + n)
                    if 0 <= b < 7:
                        totals[n] = totals[n] + (value * weights[7 * a + b][None]).reshape(TS, C)
        sides.append(jnp.concatenate(totals, axis=0))
    lines = []
    for q in (0, 1):
        totals = [jnp.zeros((TS, C), F32) for _ in range(3)]
        for k in range(3):
            whole = framed(96 * k + TS * q)
            for b in range(7):
                value = whole[5 + b : 29 + b].reshape(3, 8, C)
                for n in range(3):
                    a = 2 - k - n if q == 0 else 6 + k - n
                    if 0 <= a < 7:
                        totals[n] = totals[n] + (value * weights[7 * a + b][None]).reshape(TS, C)
        lines += totals
    lines = jnp.concatenate(lines, axis=0)
    upper = lines.astype(BF16)
    lower = (lines - upper.astype(F32)).astype(BF16)
    col = iota((1, 144), 1)
    target = col * TS
    for m in range(1, 6):
        row = m if m < 3 else tile_len - 6 + m
        target = jnp.where(col >= TS * m, (col - TS * m) * TS + row, target)
    place = one_hot(iota((CELLS, 144), 0), target)
    mixed[...] = field_mixed[...] + (dot(place, upper) + dot(place, lower))
    mixed[0:72, :] += sides[0]
    mixed[504:CELLS, :] += sides[1]

    @pl.loop(0, 6)
    def _(block):
        rows = pl.ds(pl.multiple_of(block * 96, 96), 96)
        value = mixed[rows, :]
        centred = value - jnp.mean(value, axis=1, keepdims=True)
        inverse = lax.rsqrt(jnp.mean(centred * centred, axis=1, keepdims=True) + 1e-06)
        scaled = centred * inverse
        normal[rows, :] = scaled
        rstd[rows, :] = jnp.broadcast_to(inverse, (96, 128))
        normed[rows, :] = (scaled * gain_ref[...] + nbias_ref[...]).astype(BF16)

    for copy in loads:
        copy.wait()
    grads = [jnp.where(inside, column, 0.0) for column in columns_of(c_ref)]
    for j in range(TS):
        base_ref[j * TS : j * TS + TS, :] = grads[j]
    d_branch[...] = (base_ref[...] * ls_ref[...]).astype(BF16)

    grad_in, grad_proj = [], []
    for chunk in range(3):
        hidden = slice(256 * chunk, 256 * chunk + 256)
        pre = dot(normed[...], we_ref[:, hidden]) + be_ref[hidden][None, :]
        phi = 0.5 * (1.0 + lax.erf(pre * ROOT_HALF))
        act = (pre * phi).astype(BF16)
        slope = phi + pre * INV_ROOT_TAU * jnp.exp(-0.5 * pre * pre)
        d_act = dot(d_branch[...], wp_ref[:, hidden])
        d_pre = (d_act * slope).astype(BF16)
        forward = dot_tb(act, wp_ref[:, hidden])
        backward = dot_tb(d_pre, we_ref[:, hidden])
        if chunk == 0:
            branch[...] = forward
            d_normed[...] = backward
        else:
            branch[...] += forward
            d_normed[...] += backward
        grad_in.append(dot_ta(normed[...], d_pre) * SCALE)
        grad_proj.append(dot_ta(act, d_branch[...]) * SCALE)
    grad_in = jnp.concatenate(grad_in, axis=1)
    grad_proj = jnp.concatenate(grad_proj, axis=0)
    for half in range(2):
        for x in range(2):
            gi_ref[half, x] = jnp.concatenate(
                [grad_in[24 * d : 24 * d + 24] for d in (4 * x + half, 4 * x + 2 + half)], axis=0
            ).astype(BF16)
            gp_ref[half, x] = jnp.concatenate(
                [grad_proj[96 * d : 96 * d + 96] for d in (4 * x + half, 4 * x + 2 + half)], axis=1
            ).astype(BF16)


    pl.semaphore_wait(barrier, len(peers))
    for peer in near:
        pl.semaphore_signal(near_sem, inc=1, device_id=peer, device_id_type=MESH)
    core_copies = [
        remote(gi_ref.at[1 - core], core_i, core_send.at[0], core_recv.at[0], (other, me)),
        remote(gp_ref.at[1 - core], core_p, core_send.at[1], core_recv.at[1], (other, me)),
    ]
    for copy in core_copies:
        copy.start()

    for p, (left, right) in enumerate(zip(*[iter(columns_of(x_ref))] * 2)):
        pair = []
        for j, column in ((2 * p, left), (2 * p + 1, right)):
            value = (branch[j * TS : j * TS + TS, :] + bp_ref[...]).astype(BF16).astype(F32)
            pair.append(jnp.where(inside, column + ls_ref[...] * value, 0.0))
        out_ref[:, p * PAIR : (p + 1) * PAIR] = jnp.concatenate(pair, axis=1).astype(BF16)

    d_pad[...] = jnp.zeros_like(d_pad)

    @pl.loop(0, 6)
    def _(block):
        rows = pl.ds(pl.multiple_of(block * 96, 96), 96)
        grad = d_normed[rows, :].astype(BF16).astype(F32) * gain_ref[...]
        scaled = normal[rows, :]
        mean = jnp.mean(grad, axis=1, keepdims=True)
        along = jnp.mean(grad * scaled, axis=1, keepdims=True)
        value = rstd[rows, 0:1] * (grad - mean - scaled * along)
        for j in range(4):
            d_pad[block * 4 + j + 6, 8:32] = value[j * TS : j * TS + TS]

    for copy in core_copies:
        copy.wait()
    for x in range(2):
        sum_i = gi_ref[core, x].astype(F32) + core_i[x].astype(F32)
        sum_p = gp_ref[core, x].astype(F32) + core_p[x].astype(F32)
        own_x_i[x] = sum_i
        own_x_p[x] = sum_p
        xs_i[x] = sum_i.astype(BF16)
        xs_p[x] = sum_p.astype(BF16)

    pl.semaphore_wait(near_sem, len(near))
    for peer in far:
        pl.semaphore_signal(far_sem, inc=1, device_id=peer, device_id_type=MESH)

    def x_copy(n, x, wide):
        if wide:
            return remote(xs_i.at[x], xr_i.at[n], x_send.at[n], x_recv.at[n], at_x(x))
        return remote(xs_p.at[x - 2], xr_p.at[n], x_send.at[n], x_recv.at[n], at_x(x))

    for n, x in enumerate(xs):

        @pl.when(x < 2)
        def _():
            x_copy(n, x, True).start()

        @pl.when(x >= 2)
        def _():
            x_copy(n, x, False).start()

    @pl.loop(0, 36)
    def _(at):
        whole = d_pad[at]
        for a in range(7):
            d_at[a, at] = whole[8 - a : 40 - a]

    @pl.loop(0, 10)
    def _(block):
        first = block * 3
        totals = [jnp.zeros((32, C), F32) for _ in range(3)]
        for a in range(7):
            for column in range(9):
                value = d_at[a, first + column].reshape(4, 8, C)
                for j in range(3):
                    b = j - column + 6
                    if 0 <= b < 7:
                        totals[j] = totals[j] + (value * weights[7 * a + b][None]).reshape(32, C)
        for j in range(3):
            d_ext[first + j] = totals[j]

    parts = []
    j = iota((TS, 1), 0)
    for m in range(6):
        parts.append(j * 32 + ((2 - m // 2) if m % 2 == 0 else (tile_len + 3 + m // 2)))
    middle = d_ext[3:27].reshape(TS * 32, C).astype(BF16)
    edge_rows = dot(one_hot(iota((144, TS * 32), 1), jnp.concatenate(parts, axis=0)), middle)
    parts = []
    for k in range(3):
        parts += [
            edge_rows[48 * k : 48 * k + 48],
            d_ext[2 - k, 3:27],
            d_ext[27 + k, 3:27],
        ]
    own_dh = jnp.concatenate(parts, axis=0)
    dh_ref[...] = packed(own_dh)
    own_dh = own_dh.astype(BF16)
    dh_copies = [
        remote(dh_ref, dh_lo, dh_send.at[0], dh_recv.at[0], (dp, hi)),
        remote(dh_ref, dh_hi, dh_send.at[1], dh_recv.at[1], (dp, lo)),
    ]
    for copy in dh_copies:
        copy.start()

    def regroup(wide):
        if wide:
            total = own_x_i[mx]
            for n in range(3):
                total = total + xr_i[n].astype(F32)
        else:
            total = own_x_p[mx - 2]
            for n in range(3):
                total = total + xr_p[n].astype(F32)
        total = total.astype(BF16)
        run = iota((24, 1), 0)
        height = 48 if wide else 96
        runs = None
        for part in range(8 if wide else 4):
            rows = []
            for y in range(4):
                for h in range(4):
                    if wide:
                        row = jnp.where(run % 8 == part, 24 * (y % 2) + 12 * (y // 2) + 3 * h + run // 8, -1)
                    elif part // 2 == y % 2:
                        row = jnp.where(run % 2 == part % 2, 48 * (y // 2) + 12 * h + run // 2, -1)
                    else:
                        row = jnp.full((24, 1), -1, jnp.int32)
                    rows.append(row)
            pick = one_hot(iota((384, height), 1), jnp.concatenate(rows, axis=0))
            term = dot(pick, total[:, 96 * part : 96 * part + 96])
            runs = term if runs is None else runs + term
        for y in range(4):
            at_y = [runs[96 * y + 24 * h : 96 * y + 24 * h + 24] for h in range(4)]
            y_send_buf[y] = jnp.concatenate(at_y, axis=1).astype(BF16)

    @pl.when(mx < 2)
    def _():
        for n, x in enumerate(xs):
            remote(xs_i.at[0], xr_i.at[n], x_send.at[n], x_recv.at[n], at_x(x)).wait_recv()
        regroup(True)

    @pl.when(mx >= 2)
    def _():
        for n, x in enumerate(xs):
            remote(xs_p.at[0], xr_p.at[n], x_send.at[n], x_recv.at[n], at_x(x)).wait_recv()
        regroup(False)

    y_copies = [
        remote(y_send_buf.at[y], y_recv_buf.at[n], y_send.at[n], y_recv.at[n], at_y(y))
        for n, y in enumerate(ys)
    ]
    for copy in y_copies:
        copy.start()

    for j in range(TS):
        base_ref[j * TS : j * TS + TS, :] += d_ext[3 + j, 3:27]


    spread = []
    lane = iota((1, 96), 1)
    for source in range(3):
        sender = lax.rem(me + source + TILES - 1, TILES)
        target = jnp.full((1, 96), -1, jnp.int32)
        for q in range(4):
            code = code_ref[q, sender]
            index, on_band = oriented(lane - TS * q, code, shift_ref[q, sender])
            first = jnp.where(step_ref[q, sender] == 1 - source, (code // 2) * TS, -1000)
            mine = (lane >= TS * q) & (lane < TS * q + TS)
            target = jnp.where(mine & on_band, first + index, target)
        spread.append(one_hot(iota((96, 96), 0), target))
    cell = jnp.concatenate(band_cells(tile_len), axis=0)
    to_bands = one_hot(iota((288, CELLS), 1), cell)
    for copy in y_copies:
        copy.wait()
    total = y_send_buf[my].astype(F32)
    for n in range(3):
        total = total + y_recv_buf[n].astype(F32)
    for h in range(4):
        for row in range(8):
            z_send_buf[8 * h + row] = total[3 * row : 3 * row + 3, 96 * h : 96 * h + 96].astype(BF16)
    z_copies = [
        remote(z_send_buf.at[other_z], z_recv_buf.at[n], z_send, z_recv, at_z(other_z))
        for n, other_z in enumerate(zs)
    ]
    pl.semaphore_wait(far_sem, len(far))
    for copy in z_copies:
        copy.start()

    for copy in dh_copies:
        copy.wait()
    below, above = unpacked(dh_lo), unpacked(dh_hi)
    parts = []
    for k in range(3):
        rows = slice(96 * k, 96 * k + 96)
        parts.append(
            dot(spread[0], below[rows]) + dot(spread[1], own_dh[rows]) + dot(spread[2], above[rows])
        )
    d_bands = jnp.concatenate(parts, axis=0)
    upper = d_bands.astype(BF16)
    lower = (d_bands - upper.astype(F32)).astype(BF16)
    total = base_ref[...] + (dot_ta(to_bands, upper) + dot_ta(to_bands, lower))
    inside = iota((TS, PAIR), 0) < tile_len
    for p in range(TS // 2):
        pair = [total[j * TS : j * TS + TS] for j in (2 * p, 2 * p + 1)]
        ig_ref[:, p * PAIR : (p + 1) * PAIR] = jnp.where(
            inside, jnp.concatenate(pair, axis=1), 0.0
        ).astype(BF16)

    remote(z_recv_buf, z_recv_buf, z_send, z_recv, (other, me)).wait()
    total = z_send_buf[z].astype(F32)
    for n in range(31):
        total = total + z_recv_buf[n].astype(F32)
    wg_ref[...] = jnp.concatenate([total[t : t + 1] for t in range(3)], axis=1)

    for n, x in enumerate(xs):

        @pl.when(x < 2)
        def _():
            x_copy(n, x, True).wait_send()

        @pl.when(x >= 2)
        def _():
            x_copy(n, x, False).wait_send()


def emit_kernel(out_ref, ig_ref, wg_ref, out_hbm, ig_hbm, wg_hbm, sems):
    pairs = ((out_ref, out_hbm), (ig_ref, ig_hbm), (wg_ref.at[0], wg_hbm))
    copies = [
        pltpu.make_async_copy(source, landing, sems.at[n])
        for n, (source, landing) in enumerate(pairs)
    ]
    for copy in copies:
        copy.start()
    for copy in copies:
        copy.wait()


def local(
    inputs,
    cotangent,
    tile_rows,
    neighbour_step,
    neighbour_code,
    neighbour_shift,
    conv_kernel,
    conv_bias,
    norm_gain,
    norm_bias,
    w_expand,
    b_expand,
    w_project,
    b_project,
    layer_scale,
):
    x = inputs.reshape(TS, WIDE)
    c = cotangent.reshape(TS, WIDE)
    tables = (neighbour_step.T, neighbour_code.T, neighbour_shift.T)
    dma = pltpu.SemaphoreType.DMA
    halo, field_mixed = pl.pallas_call(
        bands_kernel,
        out_shape=(
            jax.ShapeDtypeStruct((288, C), BF16),
            jax.ShapeDtypeStruct((CELLS, C), F32),
        ),
        in_specs=[SMEM] * 4 + [ANY, VMEM, VMEM],
        out_specs=(VMEM, VMEM),
        scratch_shapes=[
            pltpu.VMEM((49, 8, C), F32),
            pltpu.VMEM((7, 30, TS, C), F32),
            pltpu.VMEM((TS, WIDE), BF16),
        ]
        + [pltpu.VMEM((144, PAIR), BF16)] * 3
        + [dma, dma((2,)), dma((2,))],
        compiler_params=pltpu.CompilerParams(
            collective_id=0, has_side_effects=True, vmem_limit_bytes=BUDGET
        ),
        name="bands",
    )(tile_rows, *tables, x, conv_kernel, conv_bias.reshape(1, C))
    vm = pltpu.VMEM
    out, ig, wg = pl.pallas_call(
        main_kernel,
        out_shape=(
            jax.ShapeDtypeStruct((TS, WIDE), BF16),
            jax.ShapeDtypeStruct((TS, WIDE), BF16),
            jax.ShapeDtypeStruct((1, 288), F32),
        ),
        in_specs=[SMEM] * 4
        + [ANY, ANY]
        + [VMEM] * 5
        + [ANY, VMEM, ANY, VMEM, VMEM],
        out_specs=(VMEM,) * 3,
        scratch_shapes=[
            vm((TS, WIDE), BF16),
            vm((TS, WIDE), BF16),
            vm((C, H), BF16),
            vm((C, H), BF16),
            dma((4,)),
            vm((49, 8, C), F32),
            vm((CELLS, C), F32),
            vm((CELLS, C), F32),
            vm((CELLS, 128), F32),
            vm((CELLS, C), BF16),
            vm((CELLS, C), BF16),
            vm((CELLS, C), F32),
            vm((CELLS, C), F32),
            vm((36, 40, C), F32),
            vm((7, 36, 32, C), F32),
            vm((30, 32, C), F32),
            vm((CELLS, C), F32),
            vm((144, PAIR), BF16),
            vm((2, 2, 48, H), BF16),
            vm((2, 2, 96, PAIR), BF16),
            vm((144, PAIR), BF16),
            vm((144, PAIR), BF16),
            vm((2, 48, H), BF16),
            vm((2, 96, PAIR), BF16),
            vm((2, 48, H), BF16),
            vm((2, 96, PAIR), BF16),
            vm((3, 48, H), BF16),
            vm((3, 96, PAIR), BF16),
            vm((2, 48, H), F32),
            vm((2, 96, PAIR), F32),
            vm((4, 24, PAIR), BF16),
            vm((3, 24, PAIR), BF16),
            vm((32, 3, 96), BF16),
            vm((31, 3, 96), BF16),
        ]
        + [dma((2,))] * 4
        + [dma((3,))] * 4
        + [dma] * 2
        + [pltpu.SemaphoreType.REGULAR] * 2,
        compiler_params=pltpu.CompilerParams(
            collective_id=1, has_side_effects=True, vmem_limit_bytes=BUDGET
        ),
        name="main",
    )(
        tile_rows,
        *tables,
        x,
        c,
        halo,
        field_mixed,
        conv_kernel,
        norm_gain.reshape(1, C),
        norm_bias.reshape(1, C),
        w_expand,
        b_expand,
        w_project.T,
        b_project.reshape(1, C),
        layer_scale.reshape(1, C),
    )
    out, ig, wg = pl.pallas_call(
        emit_kernel,
        out_shape=(
            jax.ShapeDtypeStruct((TS, WIDE), BF16),
            jax.ShapeDtypeStruct((TS, WIDE), BF16),
            jax.ShapeDtypeStruct((288,), F32),
        ),
        in_specs=[VMEM] * 3,
        out_specs=(ANY,) * 3,
        scratch_shapes=[dma((3,))],
        name="emit",
    )(out, ig, wg)
    return out.reshape(1, 1, TS, WIDE), ig.reshape(1, 1, TS, WIDE), wg


def solution(mesh):
    field = P("dp", "space", None, None)
    return jax.shard_map(
        local,
        mesh=mesh,
        in_specs=(field, field) + (P(),) * 13,
        out_specs=(field, field, P(("dp", "space"))),
        check_vma=False,
    )
```

```python
import math

import jax
import jax.numpy as jnp
from jax import lax
from jax.experimental import pallas as pl
from jax.experimental.pallas import tpu as pltpu
from jax.sharding import PartitionSpec as P

C = 192
H = 768
TS = 24
CELLS = TS * TS
TILES = 64
SAMPLES = 16
WIDE = TS * C
PAIR = 2 * C
ROOT_HALF = 0.7071067811865476
INV_ROOT_TAU = 0.3989422804014327
SCALE = 1.0 / math.sqrt(SAMPLES * TILES * CELLS)
F32 = jnp.float32
BF16 = jnp.bfloat16
MESH = pl.DeviceIdType.MESH
SMEM = pl.BlockSpec(memory_space=pltpu.SMEM)
VMEM = pl.BlockSpec(memory_space=pltpu.VMEM)
ANY = pl.BlockSpec(memory_space=pl.ANY)
BUDGET = 58 << 20


def iota(shape, dim):
    return lax.broadcasted_iota(jnp.int32, shape, dim)


def one_hot(found, wanted):
    return jnp.where(found == wanted, 1.0, 0.0).astype(BF16)


def dot(a, b):
    return jnp.dot(a, b, preferred_element_type=F32)


def dot_tb(a, b):
    return lax.dot_general(a, b, (((1,), (1,)), ((), ())), preferred_element_type=F32)


def dot_ta(a, b):
    return lax.dot_general(a, b, (((0,), (0,)), ((), ())), preferred_element_type=F32)


def columns_of(ref):
    columns = []
    for p in range(TS // 2):
        pair = ref[:, p * PAIR : (p + 1) * PAIR].astype(F32)
        columns += [pair[:, :C], pair[:, C:]]
    return columns


def packed(rows):
    return jnp.concatenate([rows[:144], rows[144:]], axis=1).astype(BF16)


def unpacked(ref):
    both = ref[...].astype(F32)
    return jnp.concatenate([both[:, :C], both[:, C:]], axis=0).astype(BF16)


def band_cells(tile_len):
    i = iota((TS, 1), 0)
    parts = []
    for k in range(3):
        parts.append(i * TS + k)
        parts.append(i * TS + (tile_len - 1 - k))
        parts.append(jnp.where(i < tile_len, k * TS + i, -1))
        parts.append(jnp.where(i < tile_len, (TS - 1 - k) * TS + i, -1))
    return parts


def oriented(position, code, shift):
    unshifted = position - shift
    index = jnp.where(code % 2 == 1, TS - 1 - unshifted, unshifted)
    return index, (unshifted >= 0) & (unshifted < TS)


def bands_kernel(
    rows_ref,
    step_ref,
    code_ref,
    shift_ref,
    x_hbm,
    kern_ref,
    bias_ref,
    halo_ref,
    mixed_hbm,
    mixed_ref,
    weights,
    ext_at,
    x_ref,
    own,
    from_lo,
    from_hi,
    load,
    store,
    send,
    recv,
):
    load_x = pltpu.make_async_copy(x_hbm, x_ref, load)
    load_x.start()
    me = lax.axis_index("space")
    dp = lax.axis_index("dp")
    hi = lax.rem(me + 1, TILES)
    lo = lax.rem(me + TILES - 1, TILES)
    barrier = pltpu.get_barrier_semaphore()
    for peer in (lo, hi):
        pl.semaphore_signal(barrier, inc=1, device_id=(dp, peer), device_id_type=MESH)
    wanted = jnp.concatenate(band_cells(rows_ref[me]), axis=0)
    pick = one_hot(iota((288, CELLS), 1), wanted)
    load_x.wait()
    cells = jnp.concatenate(columns_of(x_ref), axis=0).astype(BF16)
    bands = dot(pick, cells)
    own[...] = packed(bands)
    bands = bands.astype(BF16)
    pl.semaphore_wait(barrier, 2)
    copies = []
    for n, (peer, landing) in enumerate(((hi, from_lo), (lo, from_hi))):
        copy = pltpu.make_async_remote_copy(
            src_ref=own,
            dst_ref=landing,
            send_sem=send.at[n],
            recv_sem=recv.at[n],
            device_id=(dp, peer),
            device_id_type=MESH,
        )
        copy.start()
        copies.append(copy)
    position = iota((TS, 1), 0)
    picks = []
    for source in range(3):
        parts = []
        for q in range(4):
            code = code_ref[q, me]
            index, on_band = oriented(position, code, shift_ref[q, me])
            first = jnp.where(step_ref[q, me] + 1 == source, (code // 2) * TS, -1000)
            parts.append(jnp.where(on_band, first + index, -1))
        picks.append(one_hot(iota((96, 96), 1), jnp.concatenate(parts, axis=0)))
    tile_len = rows_ref[me]
    inside = iota((TS, C), 0) < tile_len
    for t in range(49):
        weights[t] = jnp.broadcast_to(kern_ref[t // 7, t % 7 : t % 7 + 1, :], (8, C))
    blank = jnp.zeros((7, TS, C), F32)
    for k in range(3):
        ext_at[:, k] = blank
        ext_at[:, 27 + k] = blank
    for j, column in enumerate(columns_of(x_ref)):
        whole = jnp.concatenate(
            [blank[0, :8], jnp.where(inside, column, 0.0), blank[0, :8]], axis=0
        )
        for a in range(7):
            ext_at[a, 3 + j] = whole[5 + a : 29 + a]

    @pl.loop(0, 6)
    def _(block):
        first = block * 4
        totals = [jnp.broadcast_to(bias_ref[...], (TS, C)) for _ in range(4)]
        for a in range(7):
            for column in range(10):
                value = ext_at[a, first + column].reshape(3, 8, C)
                for j in range(4):
                    b = column - j
                    if 0 <= b < 7:
                        totals[j] = totals[j] + (value * weights[7 * a + b][None]).reshape(TS, C)
        for j in range(4):
            at = pl.multiple_of((first + j) * TS, TS)
            mixed_ref[pl.ds(at, TS), :] = totals[j]

    store_mixed = pltpu.make_async_copy(mixed_ref, mixed_hbm, store)
    store_mixed.start()
    for copy in copies:
        copy.wait()
    below, above = unpacked(from_lo), unpacked(from_hi)
    for k in range(3):
        rows = slice(96 * k, 96 * k + 96)
        halo_ref[rows, :] = (
            dot(picks[0], below[rows]) + dot(picks[1], bands[rows]) + dot(picks[2], above[rows])
        ).astype(BF16)
    store_mixed.wait()


def main_kernel(
    rows_ref,
    step_ref,
    code_ref,
    shift_ref,
    x_hbm,
    c_hbm,
    halo_ref,
    field_mixed,
    kern_ref,
    gain_ref,
    nbias_ref,
    we_hbm,
    be_ref,
    wp_hbm,
    bp_ref,
    ls_ref,
    out_hbm,
    ig_hbm,
    wg_ref,
    out_ref,
    ig_ref,
    store,
    x_ref,
    c_ref,
    we_ref,
    wp_ref,
    load,
    weights,
    mixed,
    normal,
    rstd,
    normed,
    d_branch,
    branch,
    d_normed,
    d_pad,
    d_at,
    d_ext,
    base_ref,
    dh_ref,
    gi_ref,
    gp_ref,
    dh_lo,
    dh_hi,
    core_i,
    core_p,
    xs_i,
    xs_p,
    xr_i,
    xr_p,
    own_x_i,
    own_x_p,
    y_send_buf,
    y_recv_buf,
    z_send_buf,
    z_recv_buf,
    dh_send,
    dh_recv,
    core_send,
    core_recv,
    x_send,
    x_recv,
    y_send,
    y_recv,
    z_send,
    z_recv,
    near_sem,
    far_sem,
):
    loads = [
        pltpu.make_async_copy(source, landing, load.at[n])
        for n, (source, landing) in enumerate(
            (
                (field_mixed, mixed),
                (x_hbm, x_ref),
                (c_hbm, c_ref),
                (we_hbm, we_ref),
                (wp_hbm, wp_ref),
            )
        )
    ]
    for copy in loads:
        copy.start()
    me = lax.axis_index("space")
    dp = lax.axis_index("dp")
    mx = dp // 4
    core = lax.rem(dp, 2)
    my = (me // 32) * 2 + lax.rem(dp // 2, 2)
    z = lax.rem(me, 32)
    hi = lax.rem(me + 1, TILES)
    lo = lax.rem(me + TILES - 1, TILES)
    other = dp + 1 - 2 * core

    def at_x(x):
        return (x * 4 + lax.rem(dp, 4), me)

    def at_y(y):
        return (mx * 4 + lax.rem(y, 2) * 2 + core, (y // 2) * 32 + z)

    def at_z(other_z):
        return (dp, me - z + other_z)

    xs = [lax.rem(mx + d, 4) for d in (1, 2, 3)]
    ys = [lax.rem(my + d, 4) for d in (1, 2, 3)]
    far_first = sorted(range(1, 32), key=lambda d: -min(d, 32 - d))
    zs = [lax.rem(z + d, 32) for d in far_first]
    near = [at_z(lax.rem(z + d, 32)) for d in (4, 28, 3, 29, 2, 30, 1, 31)]
    far = [at_z(lax.rem(z + d, 32)) for d in (8, 24)]
    peers = near + [at_y(y) for y in ys] + [at_x(x) for x in xs]
    peers += [(dp, lo), (dp, hi), (other, me)]
    barrier = pltpu.get_barrier_semaphore()
    for peer in peers:
        pl.semaphore_signal(barrier, inc=1, device_id=peer, device_id_type=MESH)

    def remote(source, landing, send, recv, peer):
        return pltpu.make_async_remote_copy(
            src_ref=source,
            dst_ref=landing,
            send_sem=send,
            recv_sem=recv,
            device_id=peer,
            device_id_type=MESH,
        )

    tile_len = rows_ref[me]
    inside = iota((TS, C), 0) < tile_len
    for t in range(49):
        weights[t] = jnp.broadcast_to(kern_ref[t // 7, t % 7 : t % 7 + 1, :], (8, C))

    halo = halo_ref[...].astype(F32)
    blank = jnp.zeros((8, C), F32)

    def framed(first):
        return jnp.concatenate([blank, halo[first : first + TS], blank], axis=0)

    sides = []
    for q in (2, 3):
        totals = [jnp.zeros((TS, C), F32) for _ in range(3)]
        for k in range(3):
            whole = framed(96 * k + TS * q)
            at = 2 - k if q == 2 else 27 + k
            for a in range(7):
                value = whole[5 + a : 29 + a].reshape(3, 8, C)
                for n in range(3):
                    b = at - (n if q == 2 else 21 + n)
                    if 0 <= b < 7:
                        totals[n] = totals[n] + (value * weights[7 * a + b][None]).reshape(TS, C)
        sides.append(jnp.concatenate(totals, axis=0))
    lines = []
    for q in (0, 1):
        totals = [jnp.zeros((TS, C), F32) for _ in range(3 if q == 0 else 9)]
        for k in range(3):
            whole = framed(96 * k + TS * q)
            for b in range(7):
                value = whole[5 + b : 29 + b].reshape(3, 8, C)
                for n in range(len(totals)):
                    a = 2 - k - n if q == 0 else 6 + k - n
                    if 0 <= a < 7:
                        totals[n] = totals[n] + (value * weights[7 * a + b][None]).reshape(TS, C)
        lines += totals
    lines = jnp.concatenate(lines, axis=0)
    upper = lines.astype(BF16)
    lower = (lines - upper.astype(F32)).astype(BF16)
    col = iota((1, 288), 1)
    target = col * TS
    for m in range(1, 12):
        row = m if m < 3 else tile_len - 6 + m
        row = jnp.where(row < TS, row, -2 * CELLS)
        target = jnp.where(col >= TS * m, (col - TS * m) * TS + row, target)
    place = one_hot(iota((CELLS, 288), 0), target)
    added = dot(place, upper) + dot(place, lower)
    loads[0].wait()
    mixed[...] += added
    mixed[0:72, :] += sides[0]
    mixed[504:CELLS, :] += sides[1]

    @pl.loop(0, 6)
    def _(block):
        rows = pl.ds(pl.multiple_of(block * 96, 96), 96)
        value = mixed[rows, :]
        centred = value - jnp.mean(value, axis=1, keepdims=True)
        inverse = lax.rsqrt(jnp.mean(centred * centred, axis=1, keepdims=True) + 1e-06)
        scaled = centred * inverse
        normal[rows, :] = scaled
        rstd[rows, :] = jnp.broadcast_to(inverse, (96, 128))
        normed[rows, :] = (scaled * gain_ref[...] + nbias_ref[...]).astype(BF16)

    for copy in loads[1:]:
        copy.wait()
    grads = [jnp.where(inside, column, 0.0) for column in columns_of(c_ref)]
    for j in range(TS):
        base_ref[j * TS : j * TS + TS, :] = grads[j]
    d_branch[...] = (base_ref[...] * ls_ref[...]).astype(BF16)

    grad_in, grad_proj = [], []
    for chunk in range(3):
        hidden = slice(256 * chunk, 256 * chunk + 256)
        pre = dot(normed[...], we_ref[:, hidden]) + be_ref[hidden][None, :]
        phi = 0.5 * (1.0 + lax.erf(pre * ROOT_HALF))
        act = (pre * phi).astype(BF16)
        slope = phi + pre * INV_ROOT_TAU * jnp.exp(-0.5 * pre * pre)
        d_act = dot(d_branch[...], wp_ref[:, hidden])
        d_pre = (d_act * slope).astype(BF16)
        forward = dot_tb(act, wp_ref[:, hidden])
        backward = dot_tb(d_pre, we_ref[:, hidden])
        if chunk == 0:
            branch[...] = forward
            d_normed[...] = backward
        else:
            branch[...] += forward
            d_normed[...] += backward
        grad_in.append(dot_ta(normed[...], d_pre) * SCALE)
        grad_proj.append(dot_ta(act, d_branch[...]) * SCALE)
    grad_in = jnp.concatenate(grad_in, axis=1)
    grad_proj = jnp.concatenate(grad_proj, axis=0)
    for half in range(2):
        for x in range(2):
            gi_ref[half, x] = jnp.concatenate(
                [grad_in[24 * d : 24 * d + 24] for d in (4 * x + half, 4 * x + 2 + half)], axis=0
            ).astype(BF16)
            gp_ref[half, x] = jnp.concatenate(
                [grad_proj[96 * d : 96 * d + 96] for d in (4 * x + half, 4 * x + 2 + half)], axis=1
            ).astype(BF16)


    pl.semaphore_wait(barrier, len(peers))
    for peer in near:
        pl.semaphore_signal(near_sem, inc=1, device_id=peer, device_id_type=MESH)
    core_copies = [
        remote(gi_ref.at[1 - core], core_i, core_send.at[0], core_recv.at[0], (other, me)),
        remote(gp_ref.at[1 - core], core_p, core_send.at[1], core_recv.at[1], (other, me)),
    ]
    for copy in core_copies:
        copy.start()

    for p, (left, right) in enumerate(zip(*[iter(columns_of(x_ref))] * 2)):
        pair = []
        for j, column in ((2 * p, left), (2 * p + 1, right)):
            value = (branch[j * TS : j * TS + TS, :] + bp_ref[...]).astype(BF16).astype(F32)
            pair.append(jnp.where(inside, column + ls_ref[...] * value, 0.0))
        out_ref[:, p * PAIR : (p + 1) * PAIR] = jnp.concatenate(pair, axis=1).astype(BF16)

    store_out = pltpu.make_async_copy(out_ref, out_hbm, store.at[0])
    store_out.start()
    d_pad[...] = jnp.zeros_like(d_pad)

    @pl.loop(0, 6)
    def _(block):
        rows = pl.ds(pl.multiple_of(block * 96, 96), 96)
        grad = d_normed[rows, :].astype(BF16).astype(F32) * gain_ref[...]
        scaled = normal[rows, :]
        mean = jnp.mean(grad, axis=1, keepdims=True)
        along = jnp.mean(grad * scaled, axis=1, keepdims=True)
        value = rstd[rows, 0:1] * (grad - mean - scaled * along)
        for j in range(4):
            d_pad[block * 4 + j + 6, 8:32] = value[j * TS : j * TS + TS]

    for copy in core_copies:
        copy.wait()
    for x in range(2):
        sum_i = gi_ref[core, x].astype(F32) + core_i[x].astype(F32)
        sum_p = gp_ref[core, x].astype(F32) + core_p[x].astype(F32)
        own_x_i[x] = sum_i
        own_x_p[x] = sum_p
        xs_i[x] = sum_i.astype(BF16)
        xs_p[x] = sum_p.astype(BF16)

    pl.semaphore_wait(near_sem, len(near))
    for peer in far:
        pl.semaphore_signal(far_sem, inc=1, device_id=peer, device_id_type=MESH)

    def x_copy(n, x, wide):
        if wide:
            return remote(xs_i.at[x], xr_i.at[n], x_send.at[n], x_recv.at[n], at_x(x))
        return remote(xs_p.at[x - 2], xr_p.at[n], x_send.at[n], x_recv.at[n], at_x(x))

    for n, x in enumerate(xs):

        @pl.when(x < 2)
        def _():
            x_copy(n, x, True).start()

        @pl.when(x >= 2)
        def _():
            x_copy(n, x, False).start()

    @pl.loop(0, 36)
    def _(at):
        whole = d_pad[at]
        for a in range(7):
            d_at[a, at] = whole[8 - a : 40 - a]

    @pl.loop(0, 10)
    def _(block):
        first = block * 3
        totals = [jnp.zeros((32, C), F32) for _ in range(3)]
        for a in range(7):
            for column in range(9):
                value = d_at[a, first + column].reshape(4, 8, C)
                for j in range(3):
                    b = j - column + 6
                    if 0 <= b < 7:
                        totals[j] = totals[j] + (value * weights[7 * a + b][None]).reshape(32, C)
        for j in range(3):
            d_ext[first + j] = totals[j]

    parts = []
    j = iota((TS, 1), 0)
    for m in range(6):
        parts.append(j * 32 + ((2 - m // 2) if m % 2 == 0 else (tile_len + 3 + m // 2)))
    middle = d_ext[3:27].reshape(TS * 32, C).astype(BF16)
    edge_rows = dot(one_hot(iota((144, TS * 32), 1), jnp.concatenate(parts, axis=0)), middle)
    parts = []
    for k in range(3):
        parts += [
            edge_rows[48 * k : 48 * k + 48],
            d_ext[2 - k, 3:27],
            d_ext[27 + k, 3:27],
        ]
    own_dh = jnp.concatenate(parts, axis=0)
    dh_ref[...] = packed(own_dh)
    own_dh = own_dh.astype(BF16)
    dh_copies = [
        remote(dh_ref, dh_lo, dh_send.at[0], dh_recv.at[0], (dp, hi)),
        remote(dh_ref, dh_hi, dh_send.at[1], dh_recv.at[1], (dp, lo)),
    ]
    for copy in dh_copies:
        copy.start()

    def regroup(wide):
        if wide:
            total = own_x_i[mx]
            for n in range(3):
                total = total + xr_i[n].astype(F32)
        else:
            total = own_x_p[mx - 2]
            for n in range(3):
                total = total + xr_p[n].astype(F32)
        total = total.astype(BF16)
        run = iota((24, 1), 0)
        height = 48 if wide else 96
        runs = None
        for part in range(8 if wide else 4):
            rows = []
            for y in range(4):
                for h in range(4):
                    if wide:
                        row = jnp.where(run % 8 == part, 24 * (y % 2) + 12 * (y // 2) + 3 * h + run // 8, -1)
                    elif part // 2 == y % 2:
                        row = jnp.where(run % 2 == part % 2, 48 * (y // 2) + 12 * h + run // 2, -1)
                    else:
                        row = jnp.full((24, 1), -1, jnp.int32)
                    rows.append(row)
            pick = one_hot(iota((384, height), 1), jnp.concatenate(rows, axis=0))
            term = dot(pick, total[:, 96 * part : 96 * part + 96])
            runs = term if runs is None else runs + term
        for y in range(4):
            at_y = [runs[96 * y + 24 * h : 96 * y + 24 * h + 24] for h in range(4)]
            y_send_buf[y] = jnp.concatenate(at_y, axis=1).astype(BF16)

    @pl.when(mx < 2)
    def _():
        for n, x in enumerate(xs):
            remote(xs_i.at[0], xr_i.at[n], x_send.at[n], x_recv.at[n], at_x(x)).wait_recv()
        regroup(True)

    @pl.when(mx >= 2)
    def _():
        for n, x in enumerate(xs):
            remote(xs_p.at[0], xr_p.at[n], x_send.at[n], x_recv.at[n], at_x(x)).wait_recv()
        regroup(False)

    y_copies = [
        remote(y_send_buf.at[y], y_recv_buf.at[n], y_send.at[n], y_recv.at[n], at_y(y))
        for n, y in enumerate(ys)
    ]
    for copy in y_copies:
        copy.start()

    for j in range(TS):
        base_ref[j * TS : j * TS + TS, :] += d_ext[3 + j, 3:27]


    spread = []
    lane = iota((1, 96), 1)
    for source in range(3):
        sender = lax.rem(me + source + TILES - 1, TILES)
        target = jnp.full((1, 96), -1, jnp.int32)
        for q in range(4):
            code = code_ref[q, sender]
            index, on_band = oriented(lane - TS * q, code, shift_ref[q, sender])
            first = jnp.where(step_ref[q, sender] == 1 - source, (code // 2) * TS, -1000)
            mine = (lane >= TS * q) & (lane < TS * q + TS)
            target = jnp.where(mine & on_band, first + index, target)
        spread.append(one_hot(iota((96, 96), 0), target))
    cell = jnp.concatenate(band_cells(tile_len), axis=0)
    to_bands = one_hot(iota((288, CELLS), 1), cell)
    for copy in y_copies:
        copy.wait()
    total = y_send_buf[my].astype(F32)
    for n in range(3):
        total = total + y_recv_buf[n].astype(F32)
    for h in range(4):
        for row in range(8):
            z_send_buf[8 * h + row] = total[3 * row : 3 * row + 3, 96 * h : 96 * h + 96].astype(BF16)
    z_copies = [
        remote(z_send_buf.at[other_z], z_recv_buf.at[n], z_send, z_recv, at_z(other_z))
        for n, other_z in enumerate(zs)
    ]
    pl.semaphore_wait(far_sem, len(far))
    for copy in z_copies:
        copy.start()

    for copy in dh_copies:
        copy.wait()
    below, above = unpacked(dh_lo), unpacked(dh_hi)
    parts = []
    for k in range(3):
        rows = slice(96 * k, 96 * k + 96)
        parts.append(
            dot(spread[0], below[rows]) + dot(spread[1], own_dh[rows]) + dot(spread[2], above[rows])
        )
    d_bands = jnp.concatenate(parts, axis=0)
    upper = d_bands.astype(BF16)
    lower = (d_bands - upper.astype(F32)).astype(BF16)
    total = base_ref[...] + (dot_ta(to_bands, upper) + dot_ta(to_bands, lower))
    inside = iota((TS, PAIR), 0) < tile_len
    for p in range(TS // 2):
        pair = [total[j * TS : j * TS + TS] for j in (2 * p, 2 * p + 1)]
        ig_ref[:, p * PAIR : (p + 1) * PAIR] = jnp.where(
            inside, jnp.concatenate(pair, axis=1), 0.0
        ).astype(BF16)

    store_ig = pltpu.make_async_copy(ig_ref, ig_hbm, store.at[1])
    store_ig.start()
    remote(z_recv_buf, z_recv_buf, z_send, z_recv, (other, me)).wait()
    total = z_send_buf[z].astype(F32)
    for n in range(31):
        total = total + z_recv_buf[n].astype(F32)
    wg_ref[...] = jnp.concatenate([total[t : t + 1] for t in range(3)], axis=1)
    store_out.wait()
    store_ig.wait()

    for n, x in enumerate(xs):

        @pl.when(x < 2)
        def _():
            x_copy(n, x, True).wait_send()

        @pl.when(x >= 2)
        def _():
            x_copy(n, x, False).wait_send()


def emit_kernel(out_ref, ig_ref, wg_ref, out_hbm, ig_hbm, wg_hbm, sems):
    pairs = ((out_ref, out_hbm), (ig_ref, ig_hbm), (wg_ref.at[0], wg_hbm))
    copies = [
        pltpu.make_async_copy(source, landing, sems.at[n])
        for n, (source, landing) in enumerate(pairs)
    ]
    for copy in copies:
        copy.start()
    for copy in copies:
        copy.wait()


def local(
    inputs,
    cotangent,
    tile_rows,
    neighbour_step,
    neighbour_code,
    neighbour_shift,
    conv_kernel,
    conv_bias,
    norm_gain,
    norm_bias,
    w_expand,
    b_expand,
    w_project,
    b_project,
    layer_scale,
):
    x = inputs.reshape(TS, WIDE)
    c = cotangent.reshape(TS, WIDE)
    tables = (neighbour_step.T, neighbour_code.T, neighbour_shift.T)
    dma = pltpu.SemaphoreType.DMA
    halo, field_mixed = pl.pallas_call(
        bands_kernel,
        out_shape=(
            jax.ShapeDtypeStruct((288, C), BF16),
            jax.ShapeDtypeStruct((CELLS, C), F32),
        ),
        in_specs=[SMEM] * 4 + [ANY, VMEM, VMEM],
        out_specs=(VMEM, ANY),
        scratch_shapes=[
            pltpu.VMEM((CELLS, C), F32),
            pltpu.VMEM((49, 8, C), F32),
            pltpu.VMEM((7, 30, TS, C), F32),
            pltpu.VMEM((TS, WIDE), BF16),
        ]
        + [pltpu.VMEM((144, PAIR), BF16)] * 3
        + [dma, dma, dma((2,)), dma((2,))],
        compiler_params=pltpu.CompilerParams(
            collective_id=0, has_side_effects=True, vmem_limit_bytes=BUDGET
        ),
        name="bands",
    )(tile_rows, *tables, x, conv_kernel, conv_bias.reshape(1, C))
    vm = pltpu.VMEM
    out, ig, wg = pl.pallas_call(
        main_kernel,
        out_shape=(
            jax.ShapeDtypeStruct((TS, WIDE), BF16),
            jax.ShapeDtypeStruct((TS, WIDE), BF16),
            jax.ShapeDtypeStruct((1, 288), F32),
        ),
        in_specs=[SMEM] * 4
        + [ANY, ANY, VMEM, ANY]
        + [VMEM] * 3
        + [ANY, VMEM, ANY, VMEM, VMEM],
        out_specs=(ANY, ANY, VMEM),
        scratch_shapes=[
            vm((TS, WIDE), BF16),
            vm((TS, WIDE), BF16),
            dma((2,)),
            vm((TS, WIDE), BF16),
            vm((TS, WIDE), BF16),
            vm((C, H), BF16),
            vm((C, H), BF16),
            dma((5,)),
            vm((49, 8, C), F32),
            vm((CELLS, C), F32),
            vm((CELLS, C), F32),
            vm((CELLS, 128), F32),
            vm((CELLS, C), BF16),
            vm((CELLS, C), BF16),
            vm((CELLS, C), F32),
            vm((CELLS, C), F32),
            vm((36, 40, C), F32),
            vm((7, 36, 32, C), F32),
            vm((30, 32, C), F32),
            vm((CELLS, C), F32),
            vm((144, PAIR), BF16),
            vm((2, 2, 48, H), BF16),
            vm((2, 2, 96, PAIR), BF16),
            vm((144, PAIR), BF16),
            vm((144, PAIR), BF16),
            vm((2, 48, H), BF16),
            vm((2, 96, PAIR), BF16),
            vm((2, 48, H), BF16),
            vm((2, 96, PAIR), BF16),
            vm((3, 48, H), BF16),
            vm((3, 96, PAIR), BF16),
            vm((2, 48, H), F32),
            vm((2, 96, PAIR), F32),
            vm((4, 24, PAIR), BF16),
            vm((3, 24, PAIR), BF16),
            vm((32, 3, 96), BF16),
            vm((31, 3, 96), BF16),
        ]
        + [dma((2,))] * 4
        + [dma((3,))] * 4
        + [dma] * 2
        + [pltpu.SemaphoreType.REGULAR] * 2,
        compiler_params=pltpu.CompilerParams(
            collective_id=1, has_side_effects=True, vmem_limit_bytes=BUDGET
        ),
        name="main",
    )(
        tile_rows,
        *tables,
        x,
        c,
        halo,
        field_mixed,
        conv_kernel,
        norm_gain.reshape(1, C),
        norm_bias.reshape(1, C),
        w_expand,
        b_expand,
        w_project.T,
        b_project.reshape(1, C),
        layer_scale.reshape(1, C),
    )
    out, ig, wg = pl.pallas_call(
        emit_kernel,
        out_shape=(
            jax.ShapeDtypeStruct((TS, WIDE), BF16),
            jax.ShapeDtypeStruct((TS, WIDE), BF16),
            jax.ShapeDtypeStruct((288,), F32),
        ),
        in_specs=[VMEM] * 3,
        out_specs=(ANY,) * 3,
        scratch_shapes=[dma((3,))],
        name="emit",
    )(out, ig, wg)
    return out.reshape(1, 1, TS, WIDE), ig.reshape(1, 1, TS, WIDE), wg


def solution(mesh):
    field = P("dp", "space", None, None)
    return jax.shard_map(
        local,
        mesh=mesh,
        in_specs=(field, field) + (P(),) * 13,
        out_specs=(field, field, P(("dp", "space"))),
        check_vma=False,
    )
```

```python
import math

import jax
import jax.numpy as jnp
from jax import lax
from jax.experimental import pallas as pl
from jax.experimental.pallas import tpu as pltpu
from jax.sharding import PartitionSpec as P

C = 192
H = 768
TS = 24
CELLS = TS * TS
TILES = 64
SAMPLES = 16
WIDE = TS * C
PAIR = 2 * C
ROOT_HALF = 0.7071067811865476
INV_ROOT_TAU = 0.3989422804014327
SCALE = 1.0 / math.sqrt(SAMPLES * TILES * CELLS)
F32 = jnp.float32
BF16 = jnp.bfloat16
MESH = pl.DeviceIdType.MESH
SMEM = pl.BlockSpec(memory_space=pltpu.SMEM)
VMEM = pl.BlockSpec(memory_space=pltpu.VMEM)
ANY = pl.BlockSpec(memory_space=pl.ANY)
BUDGET = 58 << 20


def iota(shape, dim):
    return lax.broadcasted_iota(jnp.int32, shape, dim)


def one_hot(found, wanted):
    return jnp.where(found == wanted, 1.0, 0.0).astype(BF16)


def dot(a, b):
    return jnp.dot(a, b, preferred_element_type=F32)


def dot_tb(a, b):
    return lax.dot_general(a, b, (((1,), (1,)), ((), ())), preferred_element_type=F32)


def dot_ta(a, b):
    return lax.dot_general(a, b, (((0,), (0,)), ((), ())), preferred_element_type=F32)


def columns_of(ref):
    columns = []
    for p in range(TS // 2):
        pair = ref[:, p * PAIR : (p + 1) * PAIR].astype(F32)
        columns += [pair[:, :C], pair[:, C:]]
    return columns


def packed(rows):
    return jnp.concatenate([rows[:144], rows[144:]], axis=1).astype(BF16)


def unpacked(ref):
    both = ref[...].astype(F32)
    return jnp.concatenate([both[:, :C], both[:, C:]], axis=0).astype(BF16)


def band_cells(tile_len):
    i = iota((TS, 1), 0)
    parts = []
    for k in range(3):
        parts.append(i * TS + k)
        parts.append(i * TS + (tile_len - 1 - k))
        parts.append(jnp.where(i < tile_len, k * TS + i, -1))
        parts.append(jnp.where(i < tile_len, (TS - 1 - k) * TS + i, -1))
    return parts


def oriented(position, code, shift):
    unshifted = position - shift
    index = jnp.where(code % 2 == 1, TS - 1 - unshifted, unshifted)
    return index, (unshifted >= 0) & (unshifted < TS)


def bands_kernel(
    rows_ref,
    step_ref,
    code_ref,
    shift_ref,
    x_hbm,
    kern_ref,
    bias_ref,
    halo_ref,
    mixed_hbm,
    mixed_ref,
    weights,
    ext_at,
    x_ref,
    own,
    from_lo,
    from_hi,
    load,
    store,
    send,
    recv,
):
    load_x = pltpu.make_async_copy(x_hbm, x_ref, load)
    load_x.start()
    me = lax.axis_index("space")
    dp = lax.axis_index("dp")
    hi = lax.rem(me + 1, TILES)
    lo = lax.rem(me + TILES - 1, TILES)
    barrier = pltpu.get_barrier_semaphore()
    for peer in (lo, hi):
        pl.semaphore_signal(barrier, inc=1, device_id=(dp, peer), device_id_type=MESH)
    wanted = jnp.concatenate(band_cells(rows_ref[me]), axis=0)
    pick = one_hot(iota((288, CELLS), 1), wanted)
    load_x.wait()
    cells = jnp.concatenate(columns_of(x_ref), axis=0).astype(BF16)
    bands = dot(pick, cells)
    own[...] = packed(bands)
    bands = bands.astype(BF16)
    pl.semaphore_wait(barrier, 2)
    copies = []
    for n, (peer, landing) in enumerate(((hi, from_lo), (lo, from_hi))):
        copy = pltpu.make_async_remote_copy(
            src_ref=own,
            dst_ref=landing,
            send_sem=send.at[n],
            recv_sem=recv.at[n],
            device_id=(dp, peer),
            device_id_type=MESH,
        )
        copy.start()
        copies.append(copy)
    position = iota((TS, 1), 0)
    picks = []
    for source in range(3):
        parts = []
        for q in range(4):
            code = code_ref[q, me]
            index, on_band = oriented(position, code, shift_ref[q, me])
            first = jnp.where(step_ref[q, me] + 1 == source, (code // 2) * TS, -1000)
            parts.append(jnp.where(on_band, first + index, -1))
        picks.append(one_hot(iota((96, 96), 1), jnp.concatenate(parts, axis=0)))
    tile_len = rows_ref[me]
    inside = iota((TS, C), 0) < tile_len
    for t in range(49):
        weights[t] = jnp.broadcast_to(kern_ref[t // 7, t % 7 : t % 7 + 1, :], (8, C))
    blank = jnp.zeros((7, TS, C), F32)
    for k in range(3):
        ext_at[:, k] = blank
        ext_at[:, 27 + k] = blank
    for j, column in enumerate(columns_of(x_ref)):
        whole = jnp.concatenate(
            [blank[0, :8], jnp.where(inside, column, 0.0), blank[0, :8]], axis=0
        )
        for a in range(7):
            ext_at[a, 3 + j] = whole[5 + a : 29 + a]

    @pl.loop(0, 6)
    def _(block):
        first = block * 4
        totals = [jnp.broadcast_to(bias_ref[...], (TS, C)) for _ in range(4)]
        for a in range(7):
            for column in range(10):
                value = ext_at[a, first + column].reshape(3, 8, C)
                for j in range(4):
                    b = column - j
                    if 0 <= b < 7:
                        totals[j] = totals[j] + (value * weights[7 * a + b][None]).reshape(TS, C)
        for j in range(4):
            at = pl.multiple_of((first + j) * TS, TS)
            mixed_ref[pl.ds(at, TS), :] = totals[j]

    store_mixed = pltpu.make_async_copy(mixed_ref, mixed_hbm, store)
    store_mixed.start()
    for copy in copies:
        copy.wait()
    below, above = unpacked(from_lo), unpacked(from_hi)
    for k in range(3):
        rows = slice(96 * k, 96 * k + 96)
        halo_ref[rows, :] = (
            dot(picks[0], below[rows]) + dot(picks[1], bands[rows]) + dot(picks[2], above[rows])
        ).astype(BF16)
    store_mixed.wait()


def main_kernel(
    rows_ref,
    step_ref,
    code_ref,
    shift_ref,
    x_hbm,
    c_hbm,
    halo_ref,
    field_mixed,
    kern_ref,
    gain_ref,
    nbias_ref,
    we_hbm,
    be_ref,
    wp_hbm,
    bp_ref,
    ls_ref,
    out_hbm,
    ig_hbm,
    wg_ref,
    out_ref,
    ig_ref,
    store,
    x_ref,
    c_ref,
    we_ref,
    wp_ref,
    load,
    weights,
    mixed,
    normal,
    rstd,
    normed,
    d_branch,
    branch,
    d_normed,
    d_pad,
    d_at,
    d_ext,
    base_ref,
    dh_ref,
    gi_ref,
    gp_ref,
    dh_lo,
    dh_hi,
    core_i,
    core_p,
    xs_i,
    xs_p,
    xr_i,
    xr_p,
    own_x_i,
    own_x_p,
    y_send_buf,
    y_recv_buf,
    z_send_buf,
    z_recv_buf,
    dh_send,
    dh_recv,
    core_send,
    core_recv,
    x_send,
    x_recv,
    y_send,
    y_recv,
    z_send,
    z_recv,
    near_sem,
    far_sem,
):
    loads = [
        pltpu.make_async_copy(source, landing, load.at[n])
        for n, (source, landing) in enumerate(
            (
                (field_mixed, mixed),
                (x_hbm, x_ref),
                (c_hbm, c_ref),
                (we_hbm, we_ref),
                (wp_hbm, wp_ref),
            )
        )
    ]
    for copy in loads:
        copy.start()
    me = lax.axis_index("space")
    dp = lax.axis_index("dp")
    mx = dp // 4
    core = lax.rem(dp, 2)
    my = (me // 32) * 2 + lax.rem(dp // 2, 2)
    z = lax.rem(me, 32)
    hi = lax.rem(me + 1, TILES)
    lo = lax.rem(me + TILES - 1, TILES)
    other = dp + 1 - 2 * core

    def at_x(x):
        return (x * 4 + lax.rem(dp, 4), me)

    def at_y(y):
        return (mx * 4 + lax.rem(y, 2) * 2 + core, (y // 2) * 32 + z)

    def at_z(other_z):
        return (dp, me - z + other_z)

    xs = [lax.rem(mx + d, 4) for d in (1, 2, 3)]
    ys = [lax.rem(my + d, 4) for d in (1, 2, 3)]
    far_first = sorted(range(1, 32), key=lambda d: -min(d, 32 - d))
    zs = [lax.rem(z + d, 32) for d in far_first]
    near = [at_z(lax.rem(z + d, 32)) for d in (4, 28, 3, 29, 2, 30, 1, 31)]
    far = [at_z(lax.rem(z + d, 32)) for d in (8, 24)]
    peers = near + [at_y(y) for y in ys] + [at_x(x) for x in xs]
    peers += [(dp, lo), (dp, hi), (other, me)]
    barrier = pltpu.get_barrier_semaphore()
    for peer in peers:
        pl.semaphore_signal(barrier, inc=1, device_id=peer, device_id_type=MESH)

    def remote(source, landing, send, recv, peer):
        return pltpu.make_async_remote_copy(
            src_ref=source,
            dst_ref=landing,
            send_sem=send,
            recv_sem=recv,
            device_id=peer,
            device_id_type=MESH,
        )

    tile_len = rows_ref[me]
    inside = iota((TS, C), 0) < tile_len
    for t in range(49):
        weights[t] = jnp.broadcast_to(kern_ref[t // 7, t % 7 : t % 7 + 1, :], (8, C))

    halo = halo_ref[...].astype(F32)
    blank = jnp.zeros((8, C), F32)

    def framed(first):
        return jnp.concatenate([blank, halo[first : first + TS], blank], axis=0)

    sides = []
    for q in (2, 3):
        totals = [jnp.zeros((TS, C), F32) for _ in range(3)]
        for k in range(3):
            whole = framed(96 * k + TS * q)
            at = 2 - k if q == 2 else 27 + k
            for a in range(7):
                value = whole[5 + a : 29 + a].reshape(3, 8, C)
                for n in range(3):
                    b = at - (n if q == 2 else 21 + n)
                    if 0 <= b < 7:
                        totals[n] = totals[n] + (value * weights[7 * a + b][None]).reshape(TS, C)
        sides.append(jnp.concatenate(totals, axis=0))
    lines = []
    for q in (0, 1):
        totals = [jnp.zeros((TS, C), F32) for _ in range(3 if q == 0 else 9)]
        for k in range(3):
            whole = framed(96 * k + TS * q)
            for b in range(7):
                value = whole[5 + b : 29 + b].reshape(3, 8, C)
                for n in range(len(totals)):
                    a = 2 - k - n if q == 0 else 6 + k - n
                    if 0 <= a < 7:
                        totals[n] = totals[n] + (value * weights[7 * a + b][None]).reshape(TS, C)
        lines += totals
    lines = jnp.concatenate(lines, axis=0)
    upper = lines.astype(BF16)
    lower = (lines - upper.astype(F32)).astype(BF16)
    col = iota((1, 288), 1)
    target = col * TS
    for m in range(1, 12):
        row = m if m < 3 else tile_len - 6 + m
        row = jnp.where(row < TS, row, -2 * CELLS)
        target = jnp.where(col >= TS * m, (col - TS * m) * TS + row, target)
    place = one_hot(iota((CELLS, 288), 0), target)
    added = dot(place, upper) + dot(place, lower)
    loads[0].wait()
    mixed[...] += added
    mixed[0:72, :] += sides[0]
    mixed[504:CELLS, :] += sides[1]

    @pl.loop(0, 6)
    def _(block):
        rows = pl.ds(pl.multiple_of(block * 96, 96), 96)
        value = mixed[rows, :]
        centred = value - jnp.mean(value, axis=1, keepdims=True)
        inverse = lax.rsqrt(jnp.mean(centred * centred, axis=1, keepdims=True) + 1e-06)
        scaled = centred * inverse
        normal[rows, :] = scaled
        rstd[rows, :] = jnp.broadcast_to(inverse, (96, 128))
        normed[rows, :] = (scaled * gain_ref[...] + nbias_ref[...]).astype(BF16)

    for copy in loads[1:]:
        copy.wait()
    grads = [jnp.where(inside, column, 0.0) for column in columns_of(c_ref)]
    for j in range(TS):
        base_ref[j * TS : j * TS + TS, :] = grads[j]
    d_branch[...] = (base_ref[...] * ls_ref[...]).astype(BF16)

    grad_in, grad_proj = [], []
    for chunk in range(3):
        hidden = slice(256 * chunk, 256 * chunk + 256)
        pre = dot(normed[...], we_ref[:, hidden]) + be_ref[hidden][None, :]
        phi = 0.5 * (1.0 + lax.erf(pre * ROOT_HALF))
        act = (pre * phi).astype(BF16)
        slope = phi + pre * INV_ROOT_TAU * jnp.exp(-0.5 * pre * pre)
        d_act = dot(d_branch[...], wp_ref[:, hidden])
        d_pre = (d_act * slope).astype(BF16)
        forward = dot_tb(act, wp_ref[:, hidden])
        backward = dot_tb(d_pre, we_ref[:, hidden])
        if chunk == 0:
            branch[...] = forward
            d_normed[...] = backward
        else:
            branch[...] += forward
            d_normed[...] += backward
        grad_in.append(dot_ta(normed[...], d_pre) * SCALE)
        grad_proj.append(dot_ta(act, d_branch[...]) * SCALE)
    grad_in = jnp.concatenate(grad_in, axis=1)
    grad_proj = jnp.concatenate(grad_proj, axis=0)
    for half in range(2):
        for x in range(2):
            gi_ref[half, x] = jnp.concatenate(
                [grad_in[24 * d : 24 * d + 24] for d in (4 * x + half, 4 * x + 2 + half)], axis=0
            ).astype(BF16)
            gp_ref[half, x] = jnp.concatenate(
                [grad_proj[96 * d : 96 * d + 96] for d in (4 * x + half, 4 * x + 2 + half)], axis=1
            ).astype(BF16)


    pl.semaphore_wait(barrier, len(peers))
    for peer in near:
        pl.semaphore_signal(near_sem, inc=1, device_id=peer, device_id_type=MESH)
    core_copies = [
        remote(gi_ref.at[1 - core], core_i, core_send.at[0], core_recv.at[0], (other, me)),
        remote(gp_ref.at[1 - core], core_p, core_send.at[1], core_recv.at[1], (other, me)),
    ]
    for copy in core_copies:
        copy.start()

    for p, (left, right) in enumerate(zip(*[iter(columns_of(x_ref))] * 2)):
        pair = []
        for j, column in ((2 * p, left), (2 * p + 1, right)):
            value = (branch[j * TS : j * TS + TS, :] + bp_ref[...]).astype(BF16).astype(F32)
            pair.append(jnp.where(inside, column + ls_ref[...] * value, 0.0))
        out_ref[:, p * PAIR : (p + 1) * PAIR] = jnp.concatenate(pair, axis=1).astype(BF16)

    store_out = pltpu.make_async_copy(out_ref, out_hbm, store.at[0])
    store_out.start()
    d_pad[...] = jnp.zeros_like(d_pad)

    @pl.loop(0, 6)
    def _(block):
        rows = pl.ds(pl.multiple_of(block * 96, 96), 96)
        grad = d_normed[rows, :].astype(BF16).astype(F32) * gain_ref[...]
        scaled = normal[rows, :]
        mean = jnp.mean(grad, axis=1, keepdims=True)
        along = jnp.mean(grad * scaled, axis=1, keepdims=True)
        value = rstd[rows, 0:1] * (grad - mean - scaled * along)
        for j in range(4):
            d_pad[block * 4 + j + 6, 8:32] = value[j * TS : j * TS + TS]

    for copy in core_copies:
        copy.wait()
    for x in range(2):
        sum_i = gi_ref[core, x].astype(F32) + core_i[x].astype(F32)
        sum_p = gp_ref[core, x].astype(F32) + core_p[x].astype(F32)
        own_x_i[x] = sum_i
        own_x_p[x] = sum_p
        xs_i[x] = sum_i.astype(BF16)
        xs_p[x] = sum_p.astype(BF16)

    pl.semaphore_wait(near_sem, len(near))
    for peer in far:
        pl.semaphore_signal(far_sem, inc=1, device_id=peer, device_id_type=MESH)

    def x_copy(n, x, wide):
        if wide:
            return remote(xs_i.at[x], xr_i.at[n], x_send.at[n], x_recv.at[n], at_x(x))
        return remote(xs_p.at[x - 2], xr_p.at[n], x_send.at[n], x_recv.at[n], at_x(x))

    for n, x in enumerate(xs):

        @pl.when(x < 2)
        def _():
            x_copy(n, x, True).start()

        @pl.when(x >= 2)
        def _():
            x_copy(n, x, False).start()

    @pl.loop(0, 36)
    def _(at):
        whole = d_pad[at]
        for a in range(7):
            d_at[a, at] = whole[8 - a : 40 - a]

    def convolve_back(block):
        first = block * 3
        totals = [jnp.zeros((32, C), F32) for _ in range(3)]
        for a in range(7):
            for column in range(9):
                value = d_at[a, first + column].reshape(4, 8, C)
                for j in range(3):
                    b = j - column + 6
                    if 0 <= b < 7:
                        totals[j] = totals[j] + (value * weights[7 * a + b][None]).reshape(32, C)
        for j in range(3):
            d_ext[first + j] = totals[j]

    pl.loop(0, 7)(convolve_back)

    def regroup(wide):
        if wide:
            total = own_x_i[mx]
            for n in range(3):
                total = total + xr_i[n].astype(F32)
        else:
            total = own_x_p[mx - 2]
            for n in range(3):
                total = total + xr_p[n].astype(F32)
        total = total.astype(BF16)
        run = iota((24, 1), 0)
        height = 48 if wide else 96
        runs = None
        for part in range(8 if wide else 4):
            rows = []
            for y in range(4):
                for h in range(4):
                    if wide:
                        row = jnp.where(run % 8 == part, 24 * (y % 2) + 12 * (y // 2) + 3 * h + run // 8, -1)
                    elif part // 2 == y % 2:
                        row = jnp.where(run % 2 == part % 2, 48 * (y // 2) + 12 * h + run // 2, -1)
                    else:
                        row = jnp.full((24, 1), -1, jnp.int32)
                    rows.append(row)
            pick = one_hot(iota((384, height), 1), jnp.concatenate(rows, axis=0))
            term = dot(pick, total[:, 96 * part : 96 * part + 96])
            runs = term if runs is None else runs + term
        for y in range(4):
            at_y = [runs[96 * y + 24 * h : 96 * y + 24 * h + 24] for h in range(4)]
            y_send_buf[y] = jnp.concatenate(at_y, axis=1).astype(BF16)

    @pl.when(mx < 2)
    def _():
        for n, x in enumerate(xs):
            remote(xs_i.at[0], xr_i.at[n], x_send.at[n], x_recv.at[n], at_x(x)).wait_recv()
        regroup(True)

    @pl.when(mx >= 2)
    def _():
        for n, x in enumerate(xs):
            remote(xs_p.at[0], xr_p.at[n], x_send.at[n], x_recv.at[n], at_x(x)).wait_recv()
        regroup(False)

    y_copies = [
        remote(y_send_buf.at[y], y_recv_buf.at[n], y_send.at[n], y_recv.at[n], at_y(y))
        for n, y in enumerate(ys)
    ]
    for copy in y_copies:
        copy.start()

    pl.loop(7, 10)(convolve_back)

    parts = []
    j = iota((TS, 1), 0)
    for m in range(6):
        parts.append(j * 32 + ((2 - m // 2) if m % 2 == 0 else (tile_len + 3 + m // 2)))
    middle = d_ext[3:27].reshape(TS * 32, C).astype(BF16)
    edge_rows = dot(one_hot(iota((144, TS * 32), 1), jnp.concatenate(parts, axis=0)), middle)
    parts = []
    for k in range(3):
        parts += [
            edge_rows[48 * k : 48 * k + 48],
            d_ext[2 - k, 3:27],
            d_ext[27 + k, 3:27],
        ]
    own_dh = jnp.concatenate(parts, axis=0)
    dh_ref[...] = packed(own_dh)
    own_dh = own_dh.astype(BF16)
    dh_copies = [
        remote(dh_ref, dh_lo, dh_send.at[0], dh_recv.at[0], (dp, hi)),
        remote(dh_ref, dh_hi, dh_send.at[1], dh_recv.at[1], (dp, lo)),
    ]
    for copy in dh_copies:
        copy.start()

    for copy in y_copies:
        copy.wait()
    total = y_send_buf[my].astype(F32)
    for n in range(3):
        total = total + y_recv_buf[n].astype(F32)
    for h in range(4):
        for row in range(8):
            z_send_buf[8 * h + row] = total[3 * row : 3 * row + 3, 96 * h : 96 * h + 96].astype(BF16)
    z_copies = [
        remote(z_send_buf.at[other_z], z_recv_buf.at[n], z_send, z_recv, at_z(other_z))
        for n, other_z in enumerate(zs)
    ]
    pl.semaphore_wait(far_sem, len(far))
    for copy in z_copies:
        copy.start()

    for j in range(TS):
        base_ref[j * TS : j * TS + TS, :] += d_ext[3 + j, 3:27]


    spread = []
    lane = iota((1, 96), 1)
    for source in range(3):
        sender = lax.rem(me + source + TILES - 1, TILES)
        target = jnp.full((1, 96), -1, jnp.int32)
        for q in range(4):
            code = code_ref[q, sender]
            index, on_band = oriented(lane - TS * q, code, shift_ref[q, sender])
            first = jnp.where(step_ref[q, sender] == 1 - source, (code // 2) * TS, -1000)
            mine = (lane >= TS * q) & (lane < TS * q + TS)
            target = jnp.where(mine & on_band, first + index, target)
        spread.append(one_hot(iota((96, 96), 0), target))
    cell = jnp.concatenate(band_cells(tile_len), axis=0)
    to_bands = one_hot(iota((288, CELLS), 1), cell)
    for copy in dh_copies:
        copy.wait()
    below, above = unpacked(dh_lo), unpacked(dh_hi)
    parts = []
    for k in range(3):
        rows = slice(96 * k, 96 * k + 96)
        parts.append(
            dot(spread[0], below[rows]) + dot(spread[1], own_dh[rows]) + dot(spread[2], above[rows])
        )
    d_bands = jnp.concatenate(parts, axis=0)
    upper = d_bands.astype(BF16)
    lower = (d_bands - upper.astype(F32)).astype(BF16)
    total = base_ref[...] + (dot_ta(to_bands, upper) + dot_ta(to_bands, lower))
    inside = iota((TS, PAIR), 0) < tile_len
    for p in range(TS // 2):
        pair = [total[j * TS : j * TS + TS] for j in (2 * p, 2 * p + 1)]
        ig_ref[:, p * PAIR : (p + 1) * PAIR] = jnp.where(
            inside, jnp.concatenate(pair, axis=1), 0.0
        ).astype(BF16)

    store_ig = pltpu.make_async_copy(ig_ref, ig_hbm, store.at[1])
    store_ig.start()
    remote(z_recv_buf, z_recv_buf, z_send, z_recv, (other, me)).wait()
    total = z_send_buf[z].astype(F32)
    for n in range(31):
        total = total + z_recv_buf[n].astype(F32)
    wg_ref[...] = jnp.concatenate([total[t : t + 1] for t in range(3)], axis=1)
    store_out.wait()
    store_ig.wait()

    for n, x in enumerate(xs):

        @pl.when(x < 2)
        def _():
            x_copy(n, x, True).wait_send()

        @pl.when(x >= 2)
        def _():
            x_copy(n, x, False).wait_send()


def emit_kernel(out_ref, ig_ref, wg_ref, out_hbm, ig_hbm, wg_hbm, sems):
    pairs = ((out_ref, out_hbm), (ig_ref, ig_hbm), (wg_ref.at[0], wg_hbm))
    copies = [
        pltpu.make_async_copy(source, landing, sems.at[n])
        for n, (source, landing) in enumerate(pairs)
    ]
    for copy in copies:
        copy.start()
    for copy in copies:
        copy.wait()


def local(
    inputs,
    cotangent,
    tile_rows,
    neighbour_step,
    neighbour_code,
    neighbour_shift,
    conv_kernel,
    conv_bias,
    norm_gain,
    norm_bias,
    w_expand,
    b_expand,
    w_project,
    b_project,
    layer_scale,
):
    x = inputs.reshape(TS, WIDE)
    c = cotangent.reshape(TS, WIDE)
    tables = (neighbour_step.T, neighbour_code.T, neighbour_shift.T)
    dma = pltpu.SemaphoreType.DMA
    halo, field_mixed = pl.pallas_call(
        bands_kernel,
        out_shape=(
            jax.ShapeDtypeStruct((288, C), BF16),
            jax.ShapeDtypeStruct((CELLS, C), F32),
        ),
        in_specs=[SMEM] * 4 + [ANY, VMEM, VMEM],
        out_specs=(VMEM, ANY),
        scratch_shapes=[
            pltpu.VMEM((CELLS, C), F32),
            pltpu.VMEM((49, 8, C), F32),
            pltpu.VMEM((7, 30, TS, C), F32),
            pltpu.VMEM((TS, WIDE), BF16),
        ]
        + [pltpu.VMEM((144, PAIR), BF16)] * 3
        + [dma, dma, dma((2,)), dma((2,))],
        compiler_params=pltpu.CompilerParams(
            collective_id=0, has_side_effects=True, vmem_limit_bytes=BUDGET
        ),
        name="bands",
    )(tile_rows, *tables, x, conv_kernel, conv_bias.reshape(1, C))
    vm = pltpu.VMEM
    out, ig, wg = pl.pallas_call(
        main_kernel,
        out_shape=(
            jax.ShapeDtypeStruct((TS, WIDE), BF16),
            jax.ShapeDtypeStruct((TS, WIDE), BF16),
            jax.ShapeDtypeStruct((1, 288), F32),
        ),
        in_specs=[SMEM] * 4
        + [ANY, ANY, VMEM, ANY]
        + [VMEM] * 3
        + [ANY, VMEM, ANY, VMEM, VMEM],
        out_specs=(ANY, ANY, VMEM),
        scratch_shapes=[
            vm((TS, WIDE), BF16),
            vm((TS, WIDE), BF16),
            dma((2,)),
            vm((TS, WIDE), BF16),
            vm((TS, WIDE), BF16),
            vm((C, H), BF16),
            vm((C, H), BF16),
            dma((5,)),
            vm((49, 8, C), F32),
            vm((CELLS, C), F32),
            vm((CELLS, C), F32),
            vm((CELLS, 128), F32),
            vm((CELLS, C), BF16),
            vm((CELLS, C), BF16),
            vm((CELLS, C), F32),
            vm((CELLS, C), F32),
            vm((36, 40, C), F32),
            vm((7, 36, 32, C), F32),
            vm((30, 32, C), F32),
            vm((CELLS, C), F32),
            vm((144, PAIR), BF16),
            vm((2, 2, 48, H), BF16),
            vm((2, 2, 96, PAIR), BF16),
            vm((144, PAIR), BF16),
            vm((144, PAIR), BF16),
            vm((2, 48, H), BF16),
            vm((2, 96, PAIR), BF16),
            vm((2, 48, H), BF16),
            vm((2, 96, PAIR), BF16),
            vm((3, 48, H), BF16),
            vm((3, 96, PAIR), BF16),
            vm((2, 48, H), F32),
            vm((2, 96, PAIR), F32),
            vm((4, 24, PAIR), BF16),
            vm((3, 24, PAIR), BF16),
            vm((32, 3, 96), BF16),
            vm((31, 3, 96), BF16),
        ]
        + [dma((2,))] * 4
        + [dma((3,))] * 4
        + [dma] * 2
        + [pltpu.SemaphoreType.REGULAR] * 2,
        compiler_params=pltpu.CompilerParams(
            collective_id=1, has_side_effects=True, vmem_limit_bytes=BUDGET
        ),
        name="main",
    )(
        tile_rows,
        *tables,
        x,
        c,
        halo,
        field_mixed,
        conv_kernel,
        norm_gain.reshape(1, C),
        norm_bias.reshape(1, C),
        w_expand,
        b_expand,
        w_project.T,
        b_project.reshape(1, C),
        layer_scale.reshape(1, C),
    )
    out, ig, wg = pl.pallas_call(
        emit_kernel,
        out_shape=(
            jax.ShapeDtypeStruct((TS, WIDE), BF16),
            jax.ShapeDtypeStruct((TS, WIDE), BF16),
            jax.ShapeDtypeStruct((288,), F32),
        ),
        in_specs=[VMEM] * 3,
        out_specs=(ANY,) * 3,
        scratch_shapes=[dma((3,))],
        name="emit",
    )(out, ig, wg)
    return out.reshape(1, 1, TS, WIDE), ig.reshape(1, 1, TS, WIDE), wg


def solution(mesh):
    field = P("dp", "space", None, None)
    return jax.shard_map(
        local,
        mesh=mesh,
        in_specs=(field, field) + (P(),) * 13,
        out_specs=(field, field, P(("dp", "space"))),
        check_vma=False,
    )
```
